128 devices in a mesh: gx: 8 (over x, core), gy: 16 (over y, z).
Axes of the slice: x: 4, y: 4, z: 4, core: 2. Of those that a mesh axis runs over, the one named last changes fastest.
Arguments:
- features: bfloat16 [64, 1024, 2048], P(None, 'gx', 'gy'), may hold values from -6 to 6
- cotangent: bfloat16 [64, 1024, 2048], P(None, 'gx', 'gy'), may hold values from -6 to 6
- offsets: int32 [16, 2], replicated, may hold values from -2 to 2, as said below
- adjacency: int32 [64, 128, 8], replicated, may hold values from 0 to 8191, as said below
- near_weight: bfloat16 [16, 64, 64], replicated, may hold values from -0.1875 to 0.1875
- link_weight: bfloat16 [8, 64, 64], replicated, may hold values from -0.25 to 0.25
- top_weight: bfloat16 [64, 64], replicated, may hold values from -0.75 to 0.75
- top_kernel: float32 [128, 128], replicated, may hold values from -0.5 to 0.5
Outputs:
- output: bfloat16 [64, 1024, 2048], P(None, 'gx', 'gy')
- input_grad: bfloat16 [64, 1024, 2048], P(None, 'gx', 'gy')
- near_grad: float32 [16, 64, 64], replicated
- link_grad: float32 [8, 64, 64], replicated
- top_grad: float32 [64, 64], replicated
The draws below stay inside these ranges and needn't reach their ends.
Inputs may be any that keep to these rules, and one draw needn't show every extreme that they name: `offsets`: each of the two columns takes both values -2 and 2 in some row. adjacency[i, j, l] names a level-1 cell at most 8 rows and at most 8 columns away from (i, j); row distance 8 and column distance 8 occur.
All inputs are finite; a program needn't handle non-finite values.
Results may differ from the reference program's by a relative error of at most 0.012.
Values may be sent and summed in bfloat16 or wider, within the bound.
A program may use at most 128 MiB of HBM per device.

```python
import jax
import jax.numpy as jnp
from jax import lax

WIDTH = 64
OFFSETS = 16
RADIUS = 2
LINKS = 8
FACTOR = 16
FACTOR_TOP = 8
NX = 1024
NY = 2048
M1X = 64
M1Y = 128
M2X = 8
M2Y = 16
CELLS_TOP = 128
REACH = 8


def draw_offsets(key, part):
    key = jax.random.fold_in(key, 11)
    offset_rows = jax.random.randint(key, (OFFSETS, 2), -RADIUS, RADIUS + 1)
    offset_rows = offset_rows.at[0, 0].set(RADIUS).at[1, 0].set(-RADIUS)
    offset_rows = offset_rows.at[2, 1].set(RADIUS).at[3, 1].set(-RADIUS)
    return offset_rows.astype(jnp.int32)


def draw_adjacency(key, part):
    key = jax.random.fold_in(key, 23)
    row_key, col_key = jax.random.split(key)
    row_steps = jax.random.randint(row_key, (M1X, M1Y, LINKS), -REACH, REACH + 1)
    col_steps = jax.random.randint(col_key, (M1X, M1Y, LINKS), -REACH, REACH + 1)
    row_steps = row_steps.at[:, :, 0].set(REACH).at[:, :, 1].set(-REACH)
    col_steps = col_steps.at[:, :, 0].set(REACH).at[:, :, 1].set(-REACH)
    col_steps = col_steps.at[:, :, 2].set(REACH).at[:, :, 3].set(-REACH)
    row_index = jnp.arange(M1X, dtype=jnp.int32)[:, None, None]
    col_index = jnp.arange(M1Y, dtype=jnp.int32)[None, :, None]
    target_rows = jnp.clip(row_index + row_steps, 0, M1X - 1)
    target_cols = jnp.clip(col_index + col_steps, 0, M1Y - 1)
    return (target_rows * M1Y + target_cols).astype(jnp.int32)


def levels(own_key, dims, shards, smallest, high):
    def one(axis_at, blocks):
        steps = jax.random.uniform(jax.random.fold_in(jax.random.fold_in(own_key, 6), axis_at), (blocks,), jnp.float32, smallest / len(shards), high / len(shards))
        return jnp.repeat(jnp.exp(steps), dims[axis_at] // blocks).reshape((-1,) + (1,) * (len(dims) - axis_at - 1))

    factor_of = one(*shards[0])
    for cut in shards[1:]:
        factor_of = factor_of * one(*cut)
    return factor_of


def centred(stream_key, dims, scale, reach, pieces=(), kind=jnp.bfloat16):
    gain = levels(stream_key, dims, pieces, -0.22, 0.18) if pieces else 1.0
    drawn = jax.random.normal(stream_key, dims, jnp.float32) * scale * gain
    return jnp.minimum(jnp.maximum(drawn, -reach), reach).astype(kind)


def setup_inputs(seed: int = 0) -> dict:
    arg_keys = jax.random.split(jax.random.key(seed), 9)
    features = centred(arg_keys[0], (WIDTH, NX, NY), 1.0, 6.0, ((1, 8), (2, 16)))
    cotangent = centred(arg_keys[1], (WIDTH, NX, NY), 1.0, 6.0, ((1, 8), (2, 16)))
    offsets = draw_offsets(jax.random.fold_in(arg_keys[8], 71), 0)
    adjacency = draw_adjacency(jax.random.fold_in(arg_keys[8], 71), 0)
    near_weight = centred(arg_keys[4], (OFFSETS, WIDTH, WIDTH), (OFFSETS * WIDTH) ** -0.5, 0.1875)
    link_weight = centred(arg_keys[5], (LINKS, WIDTH, WIDTH), (LINKS * WIDTH) ** -0.5, 0.25)
    top_weight = centred(arg_keys[6], (WIDTH, WIDTH), WIDTH ** -0.5, 0.75)
    top_kernel = centred(arg_keys[7], (CELLS_TOP, CELLS_TOP), CELLS_TOP ** -0.5, 0.5, (), jnp.float32)
    return dict(features=features, cotangent=cotangent, offsets=offsets, adjacency=adjacency, near_weight=near_weight, link_weight=link_weight, top_weight=top_weight, top_kernel=top_kernel)


root_scale = 0.7978845608028654
cubic_term = 0.044715


def gelu_slope(values):
    inner_arg = root_scale * (values + cubic_term * values * values * values)
    tangent = jnp.tanh(inner_arg)
    return 0.5 * (1.0 + tangent) + 0.5 * values * (1.0 - tangent * tangent) * root_scale * (1.0 + 3.0 * cubic_term * values * values)


def pool_sum(values, factor):
    channels, height, breadth = values.shape
    return values.reshape(channels, height // factor, factor, breadth // factor, factor).sum(axis=(2, 4))


def spread(values, factor):
    channels, height, breadth = values.shape
    widened = jnp.broadcast_to(values[:, :, None, :, None], (channels, height, factor, breadth, factor))
    return widened.reshape(channels, height * factor, breadth * factor)


def window(padded, row_step, col_step, height, breadth):
    zero_index = jnp.zeros((), jnp.int32)
    starts = (zero_index, (RADIUS + row_step).astype(jnp.int32), (RADIUS + col_step).astype(jnp.int32))
    return lax.dynamic_slice(padded, starts, (padded.shape[0], height, breadth))


def reference(features, cotangent, offsets, adjacency, near_weight, link_weight, top_weight, top_kernel):
    highest = lax.Precision.HIGHEST
    inputs_f32 = features.astype(jnp.float32)
    padded = jnp.pad(inputs_f32, ((0, 0), (RADIUS, RADIUS), (RADIUS, RADIUS)))
    near_f32 = near_weight.astype(jnp.float32)

    def near_step(offset_id, running):
        shifted = window(padded, offsets[offset_id, 0], offsets[offset_id, 1], NX, NY)
        return running + jnp.einsum("cxy,cd->dxy", shifted, near_f32[offset_id], precision=highest)

    near_field = lax.fori_loop(0, OFFSETS, near_step, jnp.zeros((WIDTH, NX, NY), jnp.float32))
    coarse = (pool_sum(inputs_f32, FACTOR) / FACTOR).astype(jnp.bfloat16)
    coarse_flat = coarse.astype(jnp.float32).reshape(WIDTH, M1X * M1Y)
    picked = coarse_flat[:, adjacency.reshape(-1)].reshape(WIDTH, M1X * M1Y, LINKS)
    link_f32 = link_weight.astype(jnp.float32)
    level_one = jnp.einsum("cml,lcd->dm", picked, link_f32, precision=highest).reshape(WIDTH, M1X, M1Y)
    top_coef = pool_sum(coarse.astype(jnp.float32), FACTOR_TOP) / FACTOR_TOP
    top_flat = top_coef.reshape(WIDTH, CELLS_TOP)
    top_f32 = top_weight.astype(jnp.float32)
    mixed_top = jnp.einsum("cn,cd->dn", top_flat, top_f32, precision=highest)
    level_two = jnp.dot(mixed_top, top_kernel.T, precision=highest).reshape(WIDTH, M2X, M2Y)
    hidden = near_field + spread(level_one, FACTOR) + spread(level_two, FACTOR * FACTOR_TOP)
    output = (inputs_f32 + jax.nn.gelu(hidden, approximate=True)).astype(jnp.bfloat16)

    upstream = cotangent.astype(jnp.float32)
    hidden_grad = lax.optimization_barrier((upstream * gelu_slope(hidden)).astype(jnp.bfloat16)).astype(jnp.float32)

    def weight_step(offset_id, grads):
        shifted = window(padded, offsets[offset_id, 0], offsets[offset_id, 1], NX, NY)
        return grads.at[offset_id].set(jnp.einsum("cxy,dxy->cd", shifted, hidden_grad, precision=highest))

    near_grad = lax.fori_loop(0, OFFSETS, weight_step, jnp.zeros((OFFSETS, WIDTH, WIDTH), jnp.float32))
    grad_padded = jnp.pad(hidden_grad, ((0, 0), (RADIUS, RADIUS), (RADIUS, RADIUS)))

    def back_step(offset_id, running):
        shifted = window(grad_padded, -offsets[offset_id, 0], -offsets[offset_id, 1], NX, NY)
        return running + jnp.einsum("dxy,cd->cxy", shifted, near_f32[offset_id], precision=highest)

    back_near = lax.fori_loop(0, OFFSETS, back_step, jnp.zeros((WIDTH, NX, NY), jnp.float32))
    one_grad = pool_sum(hidden_grad, FACTOR).reshape(WIDTH, M1X * M1Y)
    two_grad = pool_sum(hidden_grad, FACTOR * FACTOR_TOP).reshape(WIDTH, CELLS_TOP)
    link_grad = jnp.einsum("cml,dm->lcd", picked, one_grad, precision=highest)
    pushed = jnp.einsum("dm,lcd->cml", one_grad, link_f32, precision=highest).reshape(WIDTH, M1X * M1Y * LINKS)
    coarse_grad = jnp.zeros((WIDTH, M1X * M1Y), jnp.float32).at[:, adjacency.reshape(-1)].add(pushed)
    kernel_grad = jnp.dot(two_grad, top_kernel, precision=highest)
    top_grad = jnp.einsum("cn,dn->cd", top_flat, kernel_grad, precision=highest)
    top_coef_grad = jnp.einsum("dn,cd->cn", kernel_grad, top_f32, precision=highest).reshape(WIDTH, M2X, M2Y)
    coarse_grad = coarse_grad.reshape(WIDTH, M1X, M1Y) + spread(top_coef_grad, FACTOR_TOP) / FACTOR_TOP
    input_grad = upstream + back_near + spread(coarse_grad, FACTOR) / FACTOR
    return output, input_grad.astype(jnp.bfloat16), near_grad, link_grad, top_grad
```

```python
import functools

import jax
import jax.numpy as jnp
from jax import lax
from jax.experimental import pallas as pl
from jax.experimental.pallas import tpu as pltpu
from jax.sharding import PartitionSpec as P

C = 64
N = 128
K = 16
L = 8
CELL = 16
B = 8
W = 5
R = 2
HALO = N + 2 * R
GROUP = 4
BAND = GROUP + 2 * R
TARGETS = 640

root_scale = 0.7978845608028654
cubic_term = 0.044715

bf16 = jnp.bfloat16
f32 = jnp.float32
MESH = pl.DeviceIdType.MESH
HIGHEST = lax.Precision.HIGHEST
NT = (((1,), (1,)), ((), ()))
NN = (((1,), (0,)), ((), ()))
TN = (((0,), (0,)), ((), ()))


def dot(a, b, dims=NN, precision=None):
    return lax.dot_general(a, b, dims, preferred_element_type=f32, precision=precision)


def split_dot(a, b, dims=NN, terms=3):
    total = None
    for _ in range(terms):
        high = a.astype(bf16)
        part = dot(high, b, dims)
        total = part if total is None else total + part
        a = a - high.astype(f32)
    return total


def dot_split(a, b, dims=NN, terms=2):
    total = None
    for _ in range(terms):
        high = b.astype(bf16)
        part = dot(a, high, dims)
        total = part if total is None else total + part
        b = b - high.astype(f32)
    return total


def kernel(
    nx, ny,
    feat, cot, adj, offs, nw, lw, tw, tk,
    out, ingrad, near_out, link_out, top_out,
    fbuf, cbuf, abuf, xs, hs, xpack, hpack, xright, xleft, hright, hleft,
    wide, wide_t, w5, w5t, fwd, bwd, spread, pooled, onehot, idx,
    coarse_nb, picked, base, top1, top2, two1, two2, ctr, rctr, grads,
    rs_src, rs1, rs2_src, rs2, ag1, ag2, obuf, ibuf, one_ref, codes, code_pairs,
    load_sem, store_sem, halo_s, halo_r, hhalo_s, hhalo_r, co_s, co_r, ct_s, ct_r,
    t1_s, t1_r, t2_s, t2_r, u1_s, u1_r, u2_s, u2_r,
    r1_s, r1_r, r2_s, r2_r, a1_s, a1_r, a2_s, a2_r,
):
    gx = lax.axis_index("gx")
    gy = lax.axis_index("gy")

    def at(dx, dy):
        return (lax.rem(gx + dx + nx, nx), lax.rem(gy + dy + ny, ny))

    loads = [
        pltpu.make_async_copy(feat, fbuf, load_sem.at[0]),
        pltpu.make_async_copy(cot, cbuf, load_sem.at[1]),
        pltpu.make_async_copy(adj.at[pl.ds(gx * B, B)], abuf, load_sem.at[2]),
    ]
    for load in loads:
        load.start()

    barrier = pltpu.get_barrier_semaphore()
    for j in range(1, nx):
        pl.semaphore_signal(barrier, inc=1, device_id=at(j, 0), device_id_type=MESH)
    for j in range(1, ny):
        pl.semaphore_signal(barrier, inc=1, device_id=at(0, j), device_id_type=MESH)
    for dx in (-1, 1):
        for dy in (-1, 1):
            pl.semaphore_signal(barrier, inc=1, device_id=at(dx, dy), device_id_type=MESH)

    lane = lax.broadcasted_iota(jnp.int32, (C, N), 1)
    low = lane < C

    def build_spread(i, carry):
        rows = lax.broadcasted_iota(jnp.int32, (N, N), 0) % C
        cols = lax.broadcasted_iota(jnp.int32, (N, N), 1) // CELL + i * B
        hit = jnp.where(rows == cols, 1.0, 0.0).astype(bf16)
        spread[:, pl.ds(pl.multiple_of(i * N, N), N)] = hit
        return carry

    lax.fori_loop(0, B, build_spread, 0)
    xpack[...] = jnp.zeros_like(xpack)
    rs_src[...] = jnp.zeros_like(rs_src)
    hpack[...] = jnp.zeros_like(hpack)

    def pack_edges(block, i, pack):
        first = jnp.zeros((C, N), bf16)
        last = jnp.zeros((C, N), bf16)
        for x in range(CELL):
            turned = pltpu.roll(block[x], 2 * x, 1) if x else block[x]
            first = jnp.where((lane >= 2 * x) & (lane < 2 * x + 2), turned, first)
            spot = (2 * x - 2) % N
            last = jnp.where((lane >= spot) & (lane < spot + 2), turned, last)
        shift = 2 * CELL * lax.rem(i, 4) + 2
        half = i // 4
        pack[0, half] = pack[0, half] + pltpu.roll(first, shift, 1)
        pack[1, half] = pack[1, half] + pltpu.roll(last, shift, 1)

    loads[0].wait()

    def arrange(i, carry):
        block = jnp.swapaxes(fbuf[:, pl.ds(pl.multiple_of(i * CELL, CELL), CELL), :], 0, 1)
        xs[R, pl.ds(R + i * CELL, CELL)] = block
        total = block[0].astype(f32)
        for x in range(1, CELL):
            total = total + block[x].astype(f32)
        pooled[:, pl.ds(pl.multiple_of(i * N, N), N)] = total
        pack_edges(block, i, xpack)
        return carry

    lax.fori_loop(0, B, arrange, 0)

    def halo_copies(field, pack, right, left, send, recv):
        mid = field.at[R]
        plan = [
            (mid.at[pl.ds(R, R)], mid.at[pl.ds(R + N, R)], (-1, 0)),
            (mid.at[pl.ds(N, R)], mid.at[pl.ds(0, R)], (1, 0)),
            (pack.at[0], right.at[pl.ds(1, 2)], (0, -1)),
            (pack.at[1], left.at[pl.ds(1, 2)], (0, 1)),
            (pack.at[0, 0], right.at[3], (-1, -1)),
            (pack.at[0, 1], right.at[0], (1, -1)),
            (pack.at[1, 0], left.at[3], (-1, 1)),
            (pack.at[1, 1], left.at[0], (1, 1)),
        ]
        return [
            pltpu.make_async_remote_copy(
                src_ref=src, dst_ref=dst, send_sem=send.at[n], recv_sem=recv.at[n],
                device_id=at(*way), device_id_type=MESH,
            )
            for n, (src, dst, way) in enumerate(plan)
        ]

    def finish_halo(field, right, left):
        up, down = gx > 0, gx < nx - 1
        field[R, pl.ds(0, R)] = jnp.where(up, field[R, pl.ds(0, R)], jnp.zeros((R, C, N), bf16))
        field[R, pl.ds(R + N, R)] = jnp.where(
            down, field[R, pl.ds(R + N, R)], jnp.zeros((R, C, N), bf16)
        )
        for side, inside in ((right, gy < ny - 1), (left, gy > 0)):
            for part, there in ((0, inside & up), (1, inside), (2, inside), (3, inside & down)):
                side[part] = jnp.where(there, side[part], jnp.zeros((C, N), bf16))

        def shift(step, carry):
            for n in range(4):
                t = step * 4 + n
                place = t + (C - R)
                part = place // C
                s = 2 * lax.rem(place, C) + 2
                mixed = jnp.where(((lane - (s - 2)) & (N - 1)) < 2, left[part], right[part])
                edge = pltpu.roll(mixed, lax.rem(2 * N - s, N), 1)
                slab = field[R, t]
                field[0, t] = pltpu.roll(jnp.where(lane >= N - 2, edge, slab), 2, 1)
                field[1, t] = pltpu.roll(jnp.where(lane >= N - 1, edge, slab), 1, 1)
                field[3, t] = pltpu.roll(jnp.where(lane < 1, edge, slab), N - 1, 1)
                field[4, t] = pltpu.roll(jnp.where(lane < 2, edge, slab), N - 2, 1)
            return carry

        lax.fori_loop(0, HALO // 4, shift, 0)

    def around():
        return [(dx, dy) for dx in (-1, 0, 1) for dy in (-1, 0, 1) if (dx, dy) != (0, 0)]

    def line(axis, src, dst, send, recv):
        n = nx if axis == "gx" else ny
        me = gx if axis == "gx" else gy

        def copy(j, source, target):
            peer = lax.rem(me + j, n)
            return pltpu.make_async_remote_copy(
                src_ref=src(source(peer)), dst_ref=dst(target), send_sem=send.at[j],
                recv_sem=recv.at[j],
                device_id=(peer, gy) if axis == "gx" else (gx, peer), device_id_type=MESH,
            )

        def start():
            def step(j, carry):
                copy(j, lambda peer: peer, me).start()
                return carry

            lax.fori_loop(1, n, step, 0)

        def wait():
            def step(j, carry):
                copy(j, lambda peer: peer, lax.rem(me + n - j, n)).wait_recv()
                copy(j, lambda peer: peer, me).wait_send()
                return carry

            lax.fori_loop(1, n, step, 0)

        return start, wait

    pl.semaphore_wait(barrier, nx - 1 + ny - 1 + 4)
    xhalo = halo_copies(xs, xpack, xright, xleft, halo_s, halo_r)
    for copy in xhalo:
        copy.start()

    coarse = (split_dot(pooled[...], spread[...], NT) / CELL).astype(bf16)
    coarse_nb[4] = coarse
    coarse_copies = []
    for n, (dx, dy) in enumerate(around()):
        slot = (1 - dx) * 3 + (1 - dy)
        copy = pltpu.make_async_remote_copy(
            src_ref=coarse_nb.at[4], dst_ref=coarse_nb.at[slot], send_sem=co_s.at[n],
            recv_sem=co_r.at[n], device_id=at(dx, dy), device_id_type=MESH,
        )
        copy.start()
        coarse_copies.append(copy)
    ones = jnp.where(lax.broadcasted_iota(jnp.int32, (8, N), 1) < C, 1.0, 0.0)

    def as_row(values):
        sums = dot(ones, values, NT, HIGHEST)
        return jnp.concatenate([sums, jnp.zeros((8, N - C), f32)], axis=1)

    top1[gy] = as_row(coarse.astype(f32)) / B
    t1_start, t1_wait = line("gy", lambda p: top1.at[gy], lambda p: top1.at[p], t1_s, t1_r)
    t1_start()

    def widen(k, carry):
        block = nw[k].astype(f32)
        wide[k] = jnp.concatenate([block, block], axis=1)
        turned = block.T
        wide_t[k] = jnp.concatenate([turned, turned], axis=1)
        return carry

    lax.fori_loop(0, K, widen, 0)

    code = (offs[pl.ds(0, 1), :] + R) * W + offs[pl.ds(1, 1), :] + R

    def coded(points, stride, first):
        row = lax.broadcasted_iota(jnp.int32, (points, K), 0) * stride + first
        col = lax.broadcasted_iota(jnp.int32, (points, K), 1)
        hit = jnp.where(row == col, jnp.broadcast_to(code, (points, K)).astype(f32), 0.0)
        own = jnp.sum(hit, axis=1, keepdims=True).astype(jnp.int32)
        return jnp.broadcast_to(own, (points, N))

    codes[...] = coded(K, 1, 0)
    half = lax.broadcasted_iota(jnp.int32, (K // 2, N), 1) < C
    code_pairs[...] = jnp.where(half, coded(K // 2, 2, 0), coded(K // 2, 2, 1))

    def place(p, carry):
        plain = jnp.zeros((C, N), f32)
        turned = jnp.zeros((C, N), f32)
        for k in range(K):
            mine = codes[pl.ds(k, 1), :] == p
            plain = plain + jnp.where(mine, wide[k], 0.0)
            turned = turned + jnp.where(mine, wide_t[k], 0.0)
        w5[p] = plain.astype(bf16)
        w5t[p] = turned.astype(bf16)
        return carry

    lax.fori_loop(0, W * W, place, 0)
    nothing = jnp.zeros((C, N), bf16)

    def band(o, carry):
        for s in range(GROUP):
            for j in range(BAND // 2):
                ahead, back = [], []
                for r in (2 * j, 2 * j + 1):
                    a = r - s
                    inside = 0 <= a < W
                    ahead.append(w5t[a * W + o] if inside else nothing)
                    back.append(w5[(W - 1 - a) * W + (W - 1 - o)] if inside else nothing)
                cols = pl.ds(pl.multiple_of(o * BAND * C + j * N, N), N)
                fwd[pl.ds(s * C, C), cols] = jnp.where(low, ahead[0], ahead[1])
                bwd[pl.ds(s * C, C), cols] = jnp.where(low, back[0], back[1])
        return carry

    lax.fori_loop(0, W, band, 0)

    loads[2].wait()
    lane8 = lax.broadcasted_iota(jnp.int32, (L, N), 1)
    found = jnp.zeros((L, N), jnp.int32)
    for i in range(B):
        turned = pltpu.roll(abuf[i], lax.rem(N + i * B - gy * B, N), 1)
        found = jnp.where((lane8 >= i * B) & (lane8 < i * B + B), turned, found)
    rows = (found >> 7) - gx * B + B
    cols = (found & 127) - gy * B + B
    spot = ((rows >> 3) * 3 + (cols >> 3)) * C + (rows & 7) * B + (cols & 7)
    idx[...] = jnp.where(lane8 < C, spot, -1)

    def build_onehot(l, carry):
        target = lax.broadcasted_iota(jnp.int32, (TARGETS, N), 0)
        onehot[l] = jnp.where(target == idx[pl.ds(l, 1), :], 1.0, 0.0).astype(bf16)
        return carry

    lax.fori_loop(0, L, build_onehot, 0)

    t1_wait()
    top2[gx] = top1[:, 0, :]
    t2_start, t2_wait = line("gx", lambda p: top2.at[gx], lambda p: top2.at[p], t2_s, t2_r)
    t2_start()

    for copy in xhalo:
        copy.wait()
    finish_halo(xs, xright, xleft)

    for copy in coarse_copies:
        copy.wait()
    pieces = [
        jnp.where(low, coarse_nb[2 * j], coarse_nb[2 * j + 1] if j < 4 else nothing)
        for j in range(5)
    ]
    around_cells = jnp.concatenate(pieces, axis=1)

    def pick(l, total):
        chosen = dot(around_cells, onehot[l]).astype(bf16)
        picked[l] = chosen
        turned = lw[l].astype(f32).T.astype(bf16)
        return total + dot(turned, chosen)

    level_one = lax.fori_loop(0, L, pick, jnp.zeros((C, N), f32))
    t2_wait()
    me = gx * ny + gy
    top_all = top2[...].reshape(N, N)
    tw_f32 = tw[...].astype(f32)
    mixed = dot(tw_f32.T, top_all[:, :C], NT, HIGHEST)
    level_two = jnp.sum(mixed * tk[pl.ds(me, 1), :], axis=1, keepdims=True)
    spread_one = split_dot(level_one[:, :C], spread[pl.ds(0, C), :]) + level_two
    for i in range(B):
        base[i] = spread_one[:, i * N : (i + 1) * N]

    def banded(matrix, field, pair):
        parts = []
        for o in range(W):
            first = field[o, pl.ds(pair * 8, BAND)].reshape(BAND * C, N)
            second = field[o, pl.ds(pair * 8 + GROUP, BAND)].reshape(BAND * C, N)
            parts.append(jnp.concatenate([first, second], axis=1))
        return dot(matrix[...], jnp.concatenate(parts, axis=0))

    loads[1].wait()

    def forward(i, carry):
        rows16 = pl.ds(pl.multiple_of(i * CELL, CELL), CELL)
        upstream = jnp.swapaxes(cbuf[:, rows16, :], 0, 1)
        shared = base[i]
        actives, slopes = [], []
        total = jnp.zeros((C, N), f32)
        for half in range(2):
            near = banded(fwd, xs, i * 2 + half)
            for g in range(2):
                for s in range(GROUP):
                    x = half * 8 + g * GROUP + s
                    v = near[s * C : (s + 1) * C, g * N : (g + 1) * N] + shared
                    square = v * v
                    tangent = jnp.tanh(v * (root_scale + root_scale * cubic_term * square))
                    gate = 0.5 + 0.5 * tangent
                    actives.append(v * gate)
                    slope = gate + v * (gate - gate * gate) * (
                        2.0 * root_scale + 6.0 * root_scale * cubic_term * square
                    )
                    grad = (upstream[x].astype(f32) * slope).astype(bf16)
                    hs[R, R + i * CELL + x] = grad
                    slopes.append(grad)
                    total = total + grad.astype(f32)
        pooled[:, pl.ds(pl.multiple_of(i * N, N), N)] = total
        pack_edges(slopes, i, hpack)
        active = jnp.swapaxes(jnp.stack(actives), 0, 1)
        obuf[:, rows16, :] = (fbuf[:, rows16, :].astype(f32) + active).astype(bf16)
        pltpu.make_async_copy(
            obuf.at[:, rows16, :], out.at[:, rows16, :], store_sem.at[0, i]
        ).start()
        return carry

    lax.fori_loop(0, B, forward, 0)

    hhalo = halo_copies(hs, hpack, hright, hleft, hhalo_s, hhalo_r)
    for copy in hhalo:
        copy.start()

    one = split_dot(pooled[...], spread[...], NT)
    one_ref[...] = one
    two1[gy] = as_row(one)
    u1_start, u1_wait = line("gy", lambda p: two1.at[gy], lambda p: two1.at[p], u1_s, u1_r)
    u1_start()

    def push(l, total):
        grad = one_ref[...]
        pushed = dot_split(lw[l], grad)
        rs_src[l, pl.ds(C, C), :] = jnp.concatenate(
            [dot_split(picked[l], grad[:C, :], NT), jnp.zeros((C, N - C), f32)], axis=1
        )
        return total + split_dot(pushed, onehot[l], NT, 2)

    pushes = lax.fori_loop(0, L, push, jnp.zeros((C, TARGETS), f32))
    for j in range(5):
        ctr[j] = pushes[:, j * N : (j + 1) * N]
    push_copies = []
    for n, (dx, dy) in enumerate(around()):
        slot = (1 - dx) * 3 + (1 - dy)
        copy = pltpu.make_async_remote_copy(
            src_ref=ctr.at[(8 - slot) // 2], dst_ref=rctr.at[slot], send_sem=ct_s.at[n],
            recv_sem=ct_r.at[n], device_id=at(dx, dy), device_id_type=MESH,
        )
        copy.start()
        push_copies.append(copy)

    def weigh(step, carry):
        o = step // 2
        half = lax.rem(step, 2)
        left = jnp.concatenate(
            [
                xs[o, pl.ds(i * GROUP + half * GROUP, GROUP)].reshape(GROUP * C, N)
                for i in range(N // GROUP)
            ],
            axis=1,
        )
        right = jnp.concatenate(
            [
                hs[R, pl.ds(R + i * GROUP, GROUP)].reshape(GROUP * C, N)
                for i in range(N // GROUP)
            ],
            axis=1,
        )
        rows = pl.ds(pl.multiple_of(half * GROUP * C, GROUP * C), GROUP * C)
        grads[o, rows, :] = dot(left, right, NT)
        return carry

    lax.fori_loop(0, 4, weigh, 0)
    u1_wait()
    two2[gx] = two1[:, 0, :]
    u2_start, u2_wait = line("gx", lambda p: two2.at[gx], lambda p: two2.at[p], u2_s, u2_r)
    u2_start()
    lax.fori_loop(4, 2 * W, weigh, 0)

    def stencil_grad(p, carry):
        a = p // W
        b = lax.rem(p, W)
        part = [
            grads[b, pl.ds(pl.multiple_of((a + s) * C, C), C), pl.ds((s // 2) * N, N)]
            for s in range(GROUP)
        ]
        both = jnp.where(low, part[0] + part[2], part[1] + part[3])
        both = both + pltpu.roll(both, C, 1)
        for j in range(K // 2):
            mine = code_pairs[pl.ds(j, 1), :] == p
            rs_src[j, pl.ds(0, C), :] = jnp.where(mine, both, rs_src[j, pl.ds(0, C), :])
        return carry

    lax.fori_loop(0, W * W, stencil_grad, 0)
    rs1[gx] = rs_src[gx]
    r1_start, r1_wait = line("gx", lambda p: rs_src.at[p], lambda p: rs1.at[p], r1_s, r1_r)
    r1_start()

    for copy in hhalo:
        copy.wait()
    finish_halo(hs, hright, hleft)

    for copy in push_copies:
        copy.wait()
    evens = ctr[2]
    odds = jnp.zeros((C, N), f32)
    for slot in range(9):
        if slot == 4:
            continue
        if slot % 2 == 0:
            evens = evens + rctr[slot]
        else:
            odds = odds + rctr[slot]
    collected = evens + pltpu.roll(odds, C, 1)
    u2_wait()
    two_all = two2[...].reshape(N, N)[:, :C]
    kernel_grad = dot(tk[...], two_all, TN, HIGHEST)
    top_all = top2[...].reshape(N, N)
    top_out[...] = dot(top_all[:, :C], kernel_grad, TN, HIGHEST)
    mine = lax.broadcasted_iota(jnp.int32, (N, C), 0) == me
    kernel_row = jnp.sum(jnp.where(mine, kernel_grad, 0.0), axis=0, keepdims=True)
    top_coef_grad = jnp.sum(tw[...].astype(f32) * kernel_row, axis=1, keepdims=True)
    coarse_grad = (collected + top_coef_grad / B) / CELL
    spread_grad = split_dot(coarse_grad[:, :C], spread[pl.ds(0, C), :])
    for i in range(B):
        base[i] = spread_grad[:, i * N : (i + 1) * N]

    def backward(i, carry):
        rows16 = pl.ds(pl.multiple_of(i * CELL, CELL), CELL)
        shared = base[i]
        sums = []
        for half in range(2):
            near = banded(bwd, hs, i * 2 + half)
            for g in range(2):
                for s in range(GROUP):
                    sums.append(near[s * C : (s + 1) * C, g * N : (g + 1) * N] + shared)
        total = jnp.swapaxes(jnp.stack(sums), 0, 1)
        ibuf[:, rows16, :] = (cbuf[:, rows16, :].astype(f32) + total).astype(bf16)
        pltpu.make_async_copy(
            ibuf.at[:, rows16, :], ingrad.at[:, rows16, :], store_sem.at[1, i]
        ).start()
        return carry

    lax.fori_loop(0, 2, backward, 0)
    r1_wait()
    total = rs1[0]
    for j in range(1, nx):
        total = total + rs1[j]
    rs2_src[...] = total.reshape(ny, N // ny, N)
    rs2[gy] = rs2_src[gy]
    r2_start, r2_wait = line("gy", lambda p: rs2_src.at[p], lambda p: rs2.at[p], r2_s, r2_r)
    r2_start()
    lax.fori_loop(2, 4, backward, 0)
    r2_wait()
    total = rs2[0]
    for j in range(1, ny):
        total = total + rs2[j]
    ag1[gy] = total
    a1_start, a1_wait = line("gy", lambda p: ag1.at[gy], lambda p: ag1.at[p], a1_s, a1_r)
    a1_start()
    lax.fori_loop(4, 6, backward, 0)
    a1_wait()
    ag2[gx] = ag1[...].reshape(N, N)
    a2_start, a2_wait = line("gx", lambda p: ag2.at[gx], lambda p: ag2.at[p], a2_s, a2_r)
    a2_start()
    lax.fori_loop(6, B, backward, 0)
    a2_wait()
    for j in range(K // 2):
        near_out[2 * j] = ag2[j, pl.ds(0, C), pl.ds(0, C)]
        near_out[2 * j + 1] = ag2[j, pl.ds(0, C), pl.ds(C, C)]
        link_out[j] = ag2[j, pl.ds(C, C), pl.ds(0, C)]

    def drain(i, carry):
        rows16 = pl.ds(pl.multiple_of(i * CELL, CELL), CELL)
        pltpu.make_async_copy(
            obuf.at[:, rows16, :], out.at[:, rows16, :], store_sem.at[0, i]
        ).wait()
        pltpu.make_async_copy(
            ibuf.at[:, rows16, :], ingrad.at[:, rows16, :], store_sem.at[1, i]
        ).wait()
        return carry

    lax.fori_loop(0, B, drain, 0)


def solution(mesh):
    nx, ny = mesh.shape["gx"], mesh.shape["gy"]
    vmem = pl.BlockSpec(memory_space=pltpu.VMEM)
    anywhere = pl.BlockSpec(memory_space=pl.ANY)
    dma = pltpu.SemaphoreType.DMA

    def per_device(feat, cot, offsets, adjacency, near_w, link_w, top_w, top_k):
        scratch = [
            pltpu.VMEM((C, N, N), bf16),
            pltpu.VMEM((C, N, N), bf16),
            pltpu.VMEM((B, L, N), jnp.int32),
            pltpu.VMEM((W, HALO, C, N), bf16),
            pltpu.VMEM((W, HALO, C, N), bf16),
            pltpu.VMEM((2, 2, C, N), bf16),
            pltpu.VMEM((2, 2, C, N), bf16),
            pltpu.VMEM((4, C, N), bf16),
            pltpu.VMEM((4, C, N), bf16),
            pltpu.VMEM((4, C, N), bf16),
            pltpu.VMEM((4, C, N), bf16),
            pltpu.VMEM((K, C, N), f32),
            pltpu.VMEM((K, C, N), f32),
            pltpu.VMEM((W * W, C, N), bf16),
            pltpu.VMEM((W * W, C, N), bf16),
            pltpu.VMEM((GROUP * C, W * BAND * C), bf16),
            pltpu.VMEM((GROUP * C, W * BAND * C), bf16),
            pltpu.VMEM((N, B * N), bf16),
            pltpu.VMEM((C, B * N), f32),
            pltpu.VMEM((L, TARGETS, N), bf16),
            pltpu.VMEM((L, N), jnp.int32),
            pltpu.VMEM((9, C, N), bf16),
            pltpu.VMEM((L, C, N), bf16),
            pltpu.VMEM((B, C, N), f32),
            pltpu.VMEM((ny, 8, N), f32),
            pltpu.VMEM((nx, ny, N), f32),
            pltpu.VMEM((ny, 8, N), f32),
            pltpu.VMEM((nx, ny, N), f32),
            pltpu.VMEM((5, C, N), f32),
            pltpu.VMEM((9, C, N), f32),
            pltpu.VMEM((W, BAND * C, GROUP * C), f32),
            pltpu.VMEM((nx, N, N), f32),
            pltpu.VMEM((nx, N, N), f32),
            pltpu.VMEM((ny, N // ny, N), f32),
            pltpu.VMEM((ny, N // ny, N), f32),
            pltpu.VMEM((ny, N // ny, N), f32),
            pltpu.VMEM((nx, N, N), f32),
            pltpu.VMEM((C, N, N), bf16),
            pltpu.VMEM((C, N, N), bf16),
            pltpu.VMEM((C, N), f32),
            pltpu.VMEM((K, N), jnp.int32),
            pltpu.VMEM((K // 2, N), jnp.int32),
            dma((3,)),
            dma((2, B)),
            dma((8,)), dma((8,)), dma((8,)), dma((8,)),
            dma((8,)), dma((8,)), dma((8,)), dma((8,)),
            dma((ny,)), dma((ny,)), dma((nx,)), dma((nx,)),
            dma((ny,)), dma((ny,)), dma((nx,)), dma((nx,)),
            dma((nx,)), dma((nx,)), dma((ny,)), dma((ny,)),
            dma((ny,)), dma((ny,)), dma((nx,)), dma((nx,)),
        ]
        field = jax.ShapeDtypeStruct((C, N, N), bf16)
        return pl.pallas_call(
            functools.partial(kernel, nx, ny),
            out_shape=(
                field,
                field,
                jax.ShapeDtypeStruct((K, C, C), f32),
                jax.ShapeDtypeStruct((L, C, C), f32),
                jax.ShapeDtypeStruct((C, C), f32),
            ),
            in_specs=[
                anywhere, anywhere, anywhere,
                vmem, vmem, vmem, vmem, vmem,
            ],
            out_specs=(anywhere, anywhere, vmem, vmem, vmem),
            scratch_shapes=scratch,
            compiler_params=pltpu.CompilerParams(
                collective_id=0, has_side_effects=True, vmem_limit_bytes=60 * 2**20
            ),
        )(
            feat, cot, jnp.transpose(adjacency, (0, 2, 1)), offsets.T, near_w, link_w,
            top_w, top_k,
        )

    return jax.shard_map(
        per_device,
        mesh=mesh,
        in_specs=(P(None, "gx", "gy"), P(None, "gx", "gy"), P(), P(), P(), P(), P(), P()),
        out_specs=(P(None, "gx", "gy"), P(None, "gx", "gy"), P(), P(), P()),
        check_vma=False,
    )
```

```python
import functools

import jax
import jax.numpy as jnp
from jax import lax
from jax.experimental import pallas as pl
from jax.experimental.pallas import tpu as pltpu
from jax.sharding import PartitionSpec as P

C = 64
N = 128
K = 16
L = 8
CELL = 16
B = 8
W = 5
R = 2
HALO = N + 2 * R
GROUP = 4
BAND = GROUP + 2 * R
SLABS = 66
TARGETS = 640

root_scale = 0.7978845608028654
cubic_term = 0.044715

bf16 = jnp.bfloat16
f32 = jnp.float32
MESH = pl.DeviceIdType.MESH
HIGHEST = lax.Precision.HIGHEST
NT = (((1,), (1,)), ((), ()))
NN = (((1,), (0,)), ((), ()))
TN = (((0,), (0,)), ((), ()))


def dot(a, b, dims=NN, precision=None):
    return lax.dot_general(a, b, dims, preferred_element_type=f32, precision=precision)


def split_dot(a, b, dims=NN, terms=3):
    total = None
    for _ in range(terms):
        high = a.astype(bf16)
        part = dot(high, b, dims)
        total = part if total is None else total + part
        a = a - high.astype(f32)
    return total


def dot_split(a, b, dims=NN, terms=2):
    total = None
    for _ in range(terms):
        high = b.astype(bf16)
        part = dot(a, high, dims)
        total = part if total is None else total + part
        b = b - high.astype(f32)
    return total


def kernel(
    nx, ny,
    feat, cot, adj, offs, spots, nw, lw, tw, tk,
    obuf, ibuf, near_out, link_out, top_out,
    fbuf, cbuf, abuf, xs, hs, xpack, hpack, xright, xleft, hright, hleft,
    wide, wide_t, w5, w5t, fwd, bwd, spread, pooled, onehot, idx,
    coarse_nb, picked, base, top1, top2, two1, two2, ctr, rctr, grads,
    rs_src, rs1, rs2, ag, one_ref, codes, mover, edges, near_buf, stencil,
    load_sem, halo_s, halo_r, hhalo_s, hhalo_r, co_s, co_r, ct_s, ct_r,
    t1_s, t1_r, t2_s, t2_r, u1_s, u1_r, u2_s, u2_r,
    r1_s, r1_r, r2_s, r2_r, a1_s, a1_r,
):
    gx = lax.axis_index("gx")
    gy = lax.axis_index("gy")

    def at(dx, dy):
        return (lax.rem(gx + dx + nx, nx), lax.rem(gy + dy + ny, ny))

    loads = [
        pltpu.make_async_copy(feat, fbuf, load_sem.at[0]),
        pltpu.make_async_copy(cot, cbuf, load_sem.at[1]),
        pltpu.make_async_copy(adj.at[pl.ds(gx * B, B)], abuf, load_sem.at[2]),
    ]
    for load in loads:
        load.start()

    barrier = pltpu.get_barrier_semaphore()
    for j in range(1, nx):
        pl.semaphore_signal(barrier, inc=1, device_id=at(j, 0), device_id_type=MESH)
    for j in range(1, ny):
        pl.semaphore_signal(barrier, inc=1, device_id=at(0, j), device_id_type=MESH)
    for dx in (-1, 1):
        for dy in (-1, 1):
            pl.semaphore_signal(barrier, inc=1, device_id=at(dx, dy), device_id_type=MESH)

    lane = lax.broadcasted_iota(jnp.int32, (C, N), 1)
    low = lane < C

    def build_spread(i, carry):
        rows = lax.broadcasted_iota(jnp.int32, (N, N), 0) % C
        cols = lax.broadcasted_iota(jnp.int32, (N, N), 1) // CELL + i * B
        hit = jnp.where(rows == cols, 1.0, 0.0).astype(bf16)
        spread[:, pl.ds(pl.multiple_of(i * N, N), N)] = hit
        return carry

    lax.fori_loop(0, B, build_spread, 0)
    source = lax.broadcasted_iota(jnp.int32, (2 * N, N), 0)
    for n, o in enumerate((0, 1, 3, 4)):
        y = lax.broadcasted_iota(jnp.int32, (2 * N, N), 1) + (o - R)
        y = jnp.where(y < 0, y + N + R, jnp.where(y >= N, y + C, y))
        mover[:, n * N : (n + 1) * N] = jnp.where(source == y, 1.0, 0.0).astype(bf16)
    xpack[...] = jnp.zeros_like(xpack)
    hpack[...] = jnp.zeros_like(hpack)

    def pack_edges(block, i, pack):
        first = jnp.zeros((C, N), bf16)
        last = jnp.zeros((C, N), bf16)
        for x in range(CELL):
            turned = pltpu.roll(block[x], 2 * x, 1) if x else block[x]
            first = jnp.where((lane >= 2 * x) & (lane < 2 * x + 2), turned, first)
            spot = (2 * x - 2) % N
            last = jnp.where((lane >= spot) & (lane < spot + 2), turned, last)
        shift = 2 * CELL * lax.rem(i, 4)
        half = i // 4
        pack[0, half] = pack[0, half] + pltpu.roll(first, shift, 1)
        pack[1, half] = pack[1, half] + pltpu.roll(last, shift + 2, 1)

    loads[0].wait()

    def arrange(i, carry):
        block = jnp.swapaxes(fbuf[:, pl.ds(pl.multiple_of(i * CELL, CELL), CELL), :], 0, 1)
        xs[R, pl.ds(R + i * CELL, CELL)] = block
        total = block[0].astype(f32)
        for x in range(1, CELL):
            total = total + block[x].astype(f32)
        pooled[:, pl.ds(pl.multiple_of(i * N, N), N)] = total
        pack_edges(block, i, xpack)
        return carry

    lax.fori_loop(0, B, arrange, 0)

    def halo_copies(field, pack, right, left, send, recv):
        mid = field.at[R]
        plan = [
            (mid.at[pl.ds(R, R)], mid.at[pl.ds(R + N, R)], (-1, 0)),
            (mid.at[pl.ds(N, R)], mid.at[pl.ds(0, R)], (1, 0)),
            (pack.at[0], right.at[pl.ds(1, 2)], (0, -1)),
            (pack.at[1], left.at[pl.ds(1, 2)], (0, 1)),
            (pack.at[0, 0], right.at[3], (-1, -1)),
            (pack.at[0, 1], right.at[0], (1, -1)),
            (pack.at[1, 0], left.at[3], (-1, 1)),
            (pack.at[1, 1], left.at[0], (1, 1)),
        ]
        return [
            pltpu.make_async_remote_copy(
                src_ref=src, dst_ref=dst, send_sem=send.at[n], recv_sem=recv.at[n],
                device_id=at(*way), device_id_type=MESH,
            )
            for n, (src, dst, way) in enumerate(plan)
        ]

    def finish_halo(field, right, left):
        up, down = gx > 0, gx < nx - 1
        field[R, pl.ds(0, R)] = jnp.where(up, field[R, pl.ds(0, R)], jnp.zeros((R, C, N), bf16))
        field[R, pl.ds(R + N, R)] = jnp.where(
            down, field[R, pl.ds(R + N, R)], jnp.zeros((R, C, N), bf16)
        )
        for side, inside in ((right, gy < ny - 1), (left, gy > 0)):
            for part, there in ((0, inside & up), (1, inside), (2, inside), (3, inside & down)):
                side[part] = jnp.where(there, side[part], jnp.zeros((C, N), bf16))

        for part in range(4):
            for half in range(2):
                one, two = (left[part], pltpu.roll(right[part], C, 1))
                if half:
                    one, two = (pltpu.roll(left[part], C, 1), right[part])
                edges[2 * part + half] = jnp.where(low, one, two)

        def shift(step, carry):
            rows = []
            for n in range(SLABS):
                t = step * SLABS + n
                place = t + (C - R)
                turn = lax.rem(N - 2 * lax.rem(place, 32), N)
                rows.append(
                    jnp.concatenate([field[R, t], pltpu.roll(edges[place // 32], turn, 1)], axis=1)
                )
            moved = dot(jnp.concatenate(rows, axis=0), mover[...]).astype(bf16)
            for n, o in enumerate((0, 1, 3, 4)):
                field[o, pl.ds(step * SLABS, SLABS)] = moved[:, n * N : (n + 1) * N].reshape(
                    SLABS, C, N
                )
            return carry

        lax.fori_loop(0, HALO // SLABS, shift, 0)

    def around():
        return [(dx, dy) for dx in (-1, 0, 1) for dy in (-1, 0, 1) if (dx, dy) != (0, 0)]

    def line(axis, src, dst, send, recv):
        n = nx if axis == "gx" else ny
        me = gx if axis == "gx" else gy

        def copy(j, source, target):
            peer = lax.rem(me + j, n)
            return pltpu.make_async_remote_copy(
                src_ref=src(source(peer)), dst_ref=dst(target), send_sem=send.at[j],
                recv_sem=recv.at[j],
                device_id=(peer, gy) if axis == "gx" else (gx, peer), device_id_type=MESH,
            )

        def start():
            def step(j, carry):
                copy(j, lambda peer: peer, me).start()
                return carry

            lax.fori_loop(1, n, step, 0)

        def wait():
            def step(j, carry):
                copy(j, lambda peer: peer, lax.rem(me + n - j, n)).wait_recv()
                copy(j, lambda peer: peer, me).wait_send()
                return carry

            lax.fori_loop(1, n, step, 0)

        return start, wait

    coarse = (split_dot(pooled[...], spread[...], NT) / CELL).astype(bf16)
    coarse_nb[4] = coarse
    ones = jnp.where(lax.broadcasted_iota(jnp.int32, (8, N), 1) < C, 1.0, 0.0)

    def as_row(values):
        sums = dot(ones, values, NT, HIGHEST)
        return jnp.concatenate([sums, jnp.zeros((8, N - C), f32)], axis=1)

    top1[gy] = as_row(coarse.astype(f32)) / B

    def widen(k, carry):
        block = nw[k].astype(f32)
        wide[k] = jnp.concatenate([block, block], axis=1)
        turned = block.T
        wide_t[k] = jnp.concatenate([turned, turned], axis=1)
        return carry

    lax.fori_loop(0, K, widen, 0, unroll=4)

    code = (offs[pl.ds(0, 1), :] + R) * W + offs[pl.ds(1, 1), :] + R

    def coded(points, stride, first):
        row = lax.broadcasted_iota(jnp.int32, (points, K), 0) * stride + first
        col = lax.broadcasted_iota(jnp.int32, (points, K), 1)
        hit = jnp.where(row == col, jnp.broadcast_to(code, (points, K)).astype(f32), 0.0)
        own = jnp.sum(hit, axis=1, keepdims=True).astype(jnp.int32)
        return jnp.broadcast_to(own, (points, N))

    codes[...] = coded(K, 1, 0)

    def place(p, carry):
        plain = jnp.zeros((C, N), f32)
        turned = jnp.zeros((C, N), f32)
        for k in range(K):
            mine = codes[pl.ds(k, 1), :] == p
            plain = plain + jnp.where(mine, wide[k], 0.0)
            turned = turned + jnp.where(mine, wide_t[k], 0.0)
        w5[p] = plain.astype(bf16)
        w5t[p] = turned.astype(bf16)
        return carry

    lax.fori_loop(0, W * W, place, 0, unroll=5)
    pl.semaphore_wait(barrier, nx - 1 + ny - 1 + 4)
    xhalo = halo_copies(xs, xpack, xright, xleft, halo_s, halo_r)
    for copy in xhalo:
        copy.start()

    coarse_copies = []
    for n, (dx, dy) in enumerate(around()):
        slot = (1 - dx) * 3 + (1 - dy)
        copy = pltpu.make_async_remote_copy(
            src_ref=coarse_nb.at[4], dst_ref=coarse_nb.at[slot], send_sem=co_s.at[n],
            recv_sem=co_r.at[n], device_id=at(dx, dy), device_id_type=MESH,
        )
        copy.start()
        coarse_copies.append(copy)
    t1_start, t1_wait = line("gy", lambda p: top1.at[gy], lambda p: top1.at[p], t1_s, t1_r)
    t1_start()

    nothing = jnp.zeros((C, N), bf16)

    def band(o, carry):
        for s in range(GROUP):
            for j in range(BAND // 2):
                ahead, back = [], []
                for r in (2 * j, 2 * j + 1):
                    a = r - s
                    inside = 0 <= a < W
                    ahead.append(w5t[a * W + o] if inside else nothing)
                    back.append(w5[(W - 1 - a) * W + (W - 1 - o)] if inside else nothing)
                cols = pl.ds(pl.multiple_of(o * BAND * C + j * N, N), N)
                fwd[pl.ds(s * C, C), cols] = jnp.where(low, ahead[0], ahead[1])
                bwd[pl.ds(s * C, C), cols] = jnp.where(low, back[0], back[1])
        return carry

    lax.fori_loop(0, W, band, 0, unroll=True)

    loads[2].wait()
    lane8 = lax.broadcasted_iota(jnp.int32, (L, N), 1)
    found = jnp.zeros((L, N), jnp.int32)
    for i in range(B):
        turned = pltpu.roll(abuf[i], lax.rem(N + i * B - gy * B, N), 1)
        found = jnp.where((lane8 >= i * B) & (lane8 < i * B + B), turned, found)
    rows = (found >> 7) - gx * B + B
    cols = (found & 127) - gy * B + B
    spot = ((rows >> 3) * 3 + (cols >> 3)) * C + (rows & 7) * B + (cols & 7)
    idx[...] = jnp.where(lane8 < C, spot, -1)

    def build_onehot(l, carry):
        target = lax.broadcasted_iota(jnp.int32, (TARGETS, N), 0)
        onehot[l] = jnp.where(target == idx[pl.ds(l, 1), :], 1.0, 0.0).astype(bf16)
        return carry

    lax.fori_loop(0, L, build_onehot, 0)

    t1_wait()
    top2[gx] = top1[:, 0, :]
    t2_start, t2_wait = line("gx", lambda p: top2.at[gx], lambda p: top2.at[p], t2_s, t2_r)
    t2_start()

    for copy in xhalo:
        copy.wait()
    finish_halo(xs, xright, xleft)

    for copy in coarse_copies:
        copy.wait()
    pieces = [
        jnp.where(low, coarse_nb[2 * j], coarse_nb[2 * j + 1] if j < 4 else nothing)
        for j in range(5)
    ]
    around_cells = jnp.concatenate(pieces, axis=1)

    def pick(l, total):
        chosen = dot(around_cells, onehot[l]).astype(bf16)
        picked[l] = chosen
        turned = lw[l].astype(f32).T.astype(bf16)
        return total + dot(turned, chosen)

    level_one = lax.fori_loop(0, L, pick, jnp.zeros((C, N), f32), unroll=True)
    def banded(matrix, field, pair):
        parts = []
        for o in range(W):
            first = field[o, pl.ds(pair * 8, BAND)].reshape(BAND * C, N)
            second = field[o, pl.ds(pair * 8 + GROUP, BAND)].reshape(BAND * C, N)
            parts.append(jnp.concatenate([first, second], axis=1))
        return dot(matrix[...], jnp.concatenate(parts, axis=0))

    def near_field(pair, carry):
        near_buf[pair] = banded(fwd, xs, pair)
        return carry

    lax.fori_loop(0, N // (2 * GROUP), near_field, 0, unroll=True)
    t2_wait()
    me = gx * ny + gy
    top_all = top2[...].reshape(N, N)
    tw_f32 = tw[...].astype(f32)
    mixed = dot(tw_f32.T, top_all[:, :C], NT, HIGHEST)
    level_two = jnp.sum(mixed * tk[pl.ds(me, 1), :], axis=1, keepdims=True)
    spread_one = split_dot(level_one[:, :C], spread[pl.ds(0, C), :]) + level_two
    for i in range(B):
        base[i] = spread_one[:, i * N : (i + 1) * N]

    loads[1].wait()

    def forward(i, carry):
        rows16 = pl.ds(pl.multiple_of(i * CELL, CELL), CELL)
        upstream = jnp.swapaxes(cbuf[:, rows16, :], 0, 1)
        shared = base[i]
        actives, slopes = [], []
        total = jnp.zeros((C, N), f32)
        for half in range(2):
            for g in range(2):
                for s in range(GROUP):
                    x = half * 8 + g * GROUP + s
                    near = near_buf[i * 2 + half, pl.ds(s * C, C), pl.ds(g * N, N)]
                    v = near + shared
                    square = v * v
                    tangent = jnp.tanh(v * (root_scale + root_scale * cubic_term * square))
                    gate = 0.5 + 0.5 * tangent
                    actives.append(v * gate)
                    slope = gate + v * (gate - gate * gate) * (
                        2.0 * root_scale + 6.0 * root_scale * cubic_term * square
                    )
                    grad = (upstream[x].astype(f32) * slope).astype(bf16)
                    hs[R, R + i * CELL + x] = grad
                    slopes.append(grad)
                    total = total + grad.astype(f32)
        pooled[:, pl.ds(pl.multiple_of(i * N, N), N)] = total
        pack_edges(slopes, i, hpack)
        active = jnp.swapaxes(jnp.stack(actives), 0, 1)
        obuf[:, rows16, :] = (fbuf[:, rows16, :].astype(f32) + active).astype(bf16)
        return carry

    lax.fori_loop(0, B, forward, 0)

    hhalo = halo_copies(hs, hpack, hright, hleft, hhalo_s, hhalo_r)
    for copy in hhalo:
        copy.start()

    one = split_dot(pooled[...], spread[...], NT)
    one_ref[...] = one
    two1[gy] = as_row(one)
    u1_start, u1_wait = line("gy", lambda p: two1.at[gy], lambda p: two1.at[p], u1_s, u1_r)
    u1_start()

    left = jnp.concatenate(
        [
            jnp.concatenate(
                [xs[o, pl.ds(i * GROUP, BAND)].reshape(BAND * C, N) for i in range(N // GROUP)],
                axis=1,
            )
            for o in range(W)
        ],
        axis=0,
    )
    right = jnp.concatenate(
        [hs[R, pl.ds(R + i * GROUP, GROUP)].reshape(GROUP * C, N) for i in range(N // GROUP)],
        axis=1,
    )
    grads[...] = dot(left, right, NT).reshape(W, BAND * C, GROUP * C)
    u1_wait()
    two2[gx] = two1[:, 0, :]
    u2_start, u2_wait = line("gx", lambda p: two2.at[gx], lambda p: two2.at[p], u2_s, u2_r)
    u2_start()

    def stencil_grad(p, carry):
        a = p // W
        b = lax.rem(p, W)
        part = [
            grads[b, pl.ds(pl.multiple_of((a + s) * C, C), C), pl.ds((s // 2) * N, N)]
            for s in range(GROUP)
        ]
        both = jnp.where(low, part[0] + part[2], part[1] + part[3])
        both = both + pltpu.roll(both, C, 1)
        stencil[p] = jnp.where(low[:32], both[:32], both[32:])
        return carry

    lax.fori_loop(0, W * W, stencil_grad, 0, unroll=True)

    for k in range(K):
        rs_src[k, pl.ds(0, 32), :] = stencil[(spots[0, k] + R) * W + spots[1, k] + R].astype(bf16)

    def link_grads(l, carry):
        grad = dot_split(picked[l], one_ref[...], NT)
        for half in range(2):
            rows = [grad[(2 * half + n) * 16 : (2 * half + n + 1) * 16] for n in range(2)]
            rs_src[2 * l + half, pl.ds(32, 16), :] = jnp.concatenate(
                [rows[0][:, :C], rows[1][:, :C]], axis=1
            ).astype(bf16)
        return carry

    lax.fori_loop(0, L, link_grads, 0, unroll=True)
    rs1[gy] = rs_src[gy]
    r1_start, r1_wait = line("gy", lambda p: rs_src.at[p], lambda p: rs1.at[p], r1_s, r1_r)
    r1_start()

    def push(l, total):
        grad = one_ref[...]
        pushed = dot_split(lw[l], grad)
        return total + split_dot(pushed, onehot[l], NT, 2)

    pushes = lax.fori_loop(0, L, push, jnp.zeros((C, TARGETS), f32), unroll=True)
    for j in range(5):
        ctr[j] = pushes[:, j * N : (j + 1) * N]
    push_copies = []
    for n, (dx, dy) in enumerate(around()):
        slot = (1 - dx) * 3 + (1 - dy)
        copy = pltpu.make_async_remote_copy(
            src_ref=ctr.at[(8 - slot) // 2], dst_ref=rctr.at[slot], send_sem=ct_s.at[n],
            recv_sem=ct_r.at[n], device_id=at(dx, dy), device_id_type=MESH,
        )
        copy.start()
        push_copies.append(copy)

    for copy in hhalo:
        copy.wait()
    finish_halo(hs, hright, hleft)

    for copy in push_copies:
        copy.wait()
    evens = ctr[2]
    odds = jnp.zeros((C, N), f32)
    for slot in range(9):
        if slot == 4:
            continue
        if slot % 2 == 0:
            evens = evens + rctr[slot]
        else:
            odds = odds + rctr[slot]
    collected = evens + pltpu.roll(odds, C, 1)
    u2_wait()
    two_all = two2[...].reshape(N, N)[:, :C]
    kernel_grad = dot(tk[...], two_all, TN, HIGHEST)
    top_all = top2[...].reshape(N, N)
    top_out[...] = dot(top_all[:, :C], kernel_grad, TN, HIGHEST)
    mine = lax.broadcasted_iota(jnp.int32, (N, C), 0) == me
    kernel_row = jnp.sum(jnp.where(mine, kernel_grad, 0.0), axis=0, keepdims=True)
    top_coef_grad = jnp.sum(tw[...].astype(f32) * kernel_row, axis=1, keepdims=True)
    coarse_grad = (collected + top_coef_grad / B) / CELL
    spread_grad = split_dot(coarse_grad[:, :C], spread[pl.ds(0, C), :])
    for i in range(B):
        base[i] = spread_grad[:, i * N : (i + 1) * N]

    def backward(i, carry):
        rows16 = pl.ds(pl.multiple_of(i * CELL, CELL), CELL)
        shared = base[i]
        sums = []
        for half in range(2):
            near = banded(bwd, hs, i * 2 + half)
            for g in range(2):
                for s in range(GROUP):
                    sums.append(near[s * C : (s + 1) * C, g * N : (g + 1) * N] + shared)
        total = jnp.swapaxes(jnp.stack(sums), 0, 1)
        ibuf[:, rows16, :] = (cbuf[:, rows16, :].astype(f32) + total).astype(bf16)
        return carry

    lax.fori_loop(0, 3, backward, 0, unroll=True)
    r1_wait()
    total = rs1[0].astype(f32)
    for j in range(1, ny):
        total = total + rs1[j].astype(f32)
    rs2[gx] = total.astype(bf16)
    r2_start, r2_wait = line("gx", lambda p: rs2.at[gx], lambda p: rs2.at[p], r2_s, r2_r)
    r2_start()
    lax.fori_loop(3, 6, backward, 0, unroll=True)
    r2_wait()
    total = rs2[0].astype(f32)
    for j in range(1, nx):
        total = total + rs2[j].astype(f32)
    ag[gy] = total.astype(bf16)
    a1_start, a1_wait = line("gy", lambda p: ag.at[gy], lambda p: ag.at[p], a1_s, a1_r)
    a1_start()
    lax.fori_loop(6, B, backward, 0, unroll=True)
    a1_wait()
    for k in range(K):
        whole = ag[k].astype(f32)
        near_out[k, pl.ds(0, 32), :] = whole[:32, :C]
        near_out[k, pl.ds(32, 32), :] = pltpu.roll(whole[:32], C, 1)[:, :C]
        link_out[k // 2, pl.ds((k % 2) * 32, 16), :] = whole[32:, :C]
        link_out[k // 2, pl.ds((k % 2) * 32 + 16, 16), :] = pltpu.roll(whole[32:], C, 1)[:, :C]


def store(*refs):
    count = len(refs) // 2
    sems = refs[-1]
    copies = [
        pltpu.make_async_copy(refs[n], refs[count + n], sems.at[n]) for n in range(count)
    ]
    for copy in copies:
        copy.start()
    for copy in copies:
        copy.wait()


def solution(mesh):
    nx, ny = mesh.shape["gx"], mesh.shape["gy"]
    vmem = pl.BlockSpec(memory_space=pltpu.VMEM)
    anywhere = pl.BlockSpec(memory_space=pl.ANY)
    dma = pltpu.SemaphoreType.DMA

    def per_device(feat, cot, offsets, adjacency, near_w, link_w, top_w, top_k):
        scratch = [
            pltpu.VMEM((C, N, N), bf16),
            pltpu.VMEM((C, N, N), bf16),
            pltpu.VMEM((B, L, N), jnp.int32),
            pltpu.VMEM((W, HALO, C, N), bf16),
            pltpu.VMEM((W, HALO, C, N), bf16),
            pltpu.VMEM((2, 2, C, N), bf16),
            pltpu.VMEM((2, 2, C, N), bf16),
            pltpu.VMEM((4, C, N), bf16),
            pltpu.VMEM((4, C, N), bf16),
            pltpu.VMEM((4, C, N), bf16),
            pltpu.VMEM((4, C, N), bf16),
            pltpu.VMEM((K, C, N), f32),
            pltpu.VMEM((K, C, N), f32),
            pltpu.VMEM((W * W, C, N), bf16),
            pltpu.VMEM((W * W, C, N), bf16),
            pltpu.VMEM((GROUP * C, W * BAND * C), bf16),
            pltpu.VMEM((GROUP * C, W * BAND * C), bf16),
            pltpu.VMEM((N, B * N), bf16),
            pltpu.VMEM((C, B * N), f32),
            pltpu.VMEM((L, TARGETS, N), bf16),
            pltpu.VMEM((L, N), jnp.int32),
            pltpu.VMEM((9, C, N), bf16),
            pltpu.VMEM((L, C, N), bf16),
            pltpu.VMEM((B, C, N), f32),
            pltpu.VMEM((ny, 8, N), f32),
            pltpu.VMEM((nx, ny, N), f32),
            pltpu.VMEM((ny, 8, N), f32),
            pltpu.VMEM((nx, ny, N), f32),
            pltpu.VMEM((5, C, N), f32),
            pltpu.VMEM((9, C, N), f32),
            pltpu.VMEM((W, BAND * C, GROUP * C), f32),
            pltpu.VMEM((ny, 48, N), bf16),
            pltpu.VMEM((ny, 48, N), bf16),
            pltpu.VMEM((nx, 48, N), bf16),
            pltpu.VMEM((ny, 48, N), bf16),
            pltpu.VMEM((C, N), f32),
            pltpu.VMEM((K, N), jnp.int32),
            pltpu.VMEM((2 * N, 4 * N), bf16),
            pltpu.VMEM((8, C, N), bf16),
            pltpu.VMEM((N // (2 * GROUP), GROUP * C, 2 * N), f32),
            pltpu.VMEM((W * W, 32, N), f32),
            dma((3,)),
            dma((8,)), dma((8,)), dma((8,)), dma((8,)),
            dma((8,)), dma((8,)), dma((8,)), dma((8,)),
            dma((ny,)), dma((ny,)), dma((nx,)), dma((nx,)),
            dma((ny,)), dma((ny,)), dma((nx,)), dma((nx,)),
            dma((ny,)), dma((ny,)), dma((nx,)), dma((nx,)), dma((ny,)), dma((ny,)),
        ]
        results = (
            ((C, N, N), bf16),
            ((C, N, N), bf16),
            ((K, C, C), f32),
            ((L, C, C), f32),
            ((C, C), f32),
        )
        held = pl.pallas_call(
            functools.partial(kernel, nx, ny),
            out_shape=[pltpu.VMEM(*result) for result in results],
            in_specs=[
                anywhere, anywhere, anywhere,
                vmem,
                pl.BlockSpec(memory_space=pltpu.SMEM),
                vmem, vmem, vmem, vmem,
            ],
            out_specs=[vmem] * 5,
            scratch_shapes=scratch,
            compiler_params=pltpu.CompilerParams(
                collective_id=0, has_side_effects=True, vmem_limit_bytes=54 * 2**20
            ),
        )(
            feat, cot, jnp.transpose(adjacency, (0, 2, 1)), offsets.T, offsets.T, near_w, link_w,
            top_w, top_k,
        )
        return pl.pallas_call(
            store,
            out_shape=[jax.ShapeDtypeStruct(*result) for result in results],
            in_specs=[vmem] * 5,
            out_specs=[anywhere] * 5,
            scratch_shapes=[dma((5,))],
            compiler_params=pltpu.CompilerParams(vmem_limit_bytes=2**20),
        )(*[pltpu.with_memory_space_constraint(value, pltpu.VMEM) for value in held])

    return jax.shard_map(
        per_device,
        mesh=mesh,
        in_specs=(P(None, "gx", "gy"), P(None, "gx", "gy"), P(), P(), P(), P(), P(), P()),
        out_specs=(P(None, "gx", "gy"), P(None, "gx", "gy"), P(), P(), P()),
        check_vma=False,
    )
```

```python
import functools

import jax
import jax.numpy as jnp
from jax import lax
from jax.experimental import pallas as pl
from jax.experimental.pallas import tpu as pltpu
from jax.sharding import PartitionSpec as P

C = 64
N = 128
K = 16
L = 8
CELL = 16
B = 8
W = 5
R = 2
HALO = N + 2 * R
GROUP = 4
BAND = GROUP + 2 * R
SLABS = 66
TARGETS = 640

root_scale = 0.7978845608028654
cubic_term = 0.044715

bf16 = jnp.bfloat16
f32 = jnp.float32
MESH = pl.DeviceIdType.MESH
HIGHEST = lax.Precision.HIGHEST
NT = (((1,), (1,)), ((), ()))
NN = (((1,), (0,)), ((), ()))
TN = (((0,), (0,)), ((), ()))


def dot(a, b, dims=NN, precision=None):
    return lax.dot_general(a, b, dims, preferred_element_type=f32, precision=precision)


def split_dot(a, b, dims=NN, terms=3):
    total = None
    for _ in range(terms):
        high = a.astype(bf16)
        part = dot(high, b, dims)
        total = part if total is None else total + part
        a = a - high.astype(f32)
    return total


def dot_split(a, b, dims=NN, terms=2):
    total = None
    for _ in range(terms):
        high = b.astype(bf16)
        part = dot(a, high, dims)
        total = part if total is None else total + part
        b = b - high.astype(f32)
    return total


def kernel(
    nx, ny,
    feat, cot, adj, offs, spots, nw, lw, tw, tk,
    obuf, ibuf, near_out, link_out, top_out,
    fbuf, cbuf, abuf, xs, hs, xpack, hpack, xright, xleft, hright, hleft,
    wide, wide_t, w5, w5t, fwd, bwd, spread, pooled, onehot, idx,
    coarse_nb, picked, base, top1, top2, two1, two2, ctr, rctr, grads,
    rs_src, rs1, rs2, ag, one_ref, codes, mover, edges, near_buf, stencil,
    load_sem, halo_s, halo_r, hhalo_s, hhalo_r, co_s, co_r, ct_s, ct_r,
    t1_s, t1_r, t2_s, t2_r, u1_s, u1_r, u2_s, u2_r,
    r1_s, r1_r, r2_s, r2_r, a1_s, a1_r,
):
    gx = lax.axis_index("gx")
    gy = lax.axis_index("gy")

    def at(dx, dy):
        return (lax.rem(gx + dx + nx, nx), lax.rem(gy + dy + ny, ny))

    loads = [
        pltpu.make_async_copy(feat, fbuf, load_sem.at[0]),
        pltpu.make_async_copy(cot, cbuf, load_sem.at[1]),
        pltpu.make_async_copy(adj.at[pl.ds(gx * B, B)], abuf, load_sem.at[2]),
    ]
    for load in loads:
        load.start()

    barrier = pltpu.get_barrier_semaphore()
    for j in range(1, nx):
        pl.semaphore_signal(barrier, inc=1, device_id=at(j, 0), device_id_type=MESH)
    for j in range(1, ny):
        pl.semaphore_signal(barrier, inc=1, device_id=at(0, j), device_id_type=MESH)
    for dx in (-1, 1):
        for dy in (-1, 1):
            pl.semaphore_signal(barrier, inc=1, device_id=at(dx, dy), device_id_type=MESH)

    lane = lax.broadcasted_iota(jnp.int32, (C, N), 1)
    low = lane < C

    def build_spread(i, carry):
        rows = lax.broadcasted_iota(jnp.int32, (N, N), 0) % C
        cols = lax.broadcasted_iota(jnp.int32, (N, N), 1) // CELL + i * B
        hit = jnp.where(rows == cols, 1.0, 0.0).astype(bf16)
        spread[:, pl.ds(pl.multiple_of(i * N, N), N)] = hit
        return carry

    lax.fori_loop(0, B, build_spread, 0)
    xpack[...] = jnp.zeros_like(xpack)

    def pack_edges(block, i, pack):
        first = jnp.zeros((C, N), bf16)
        last = jnp.zeros((C, N), bf16)
        for x in range(CELL):
            turned = pltpu.roll(block[x], 2 * x, 1) if x else block[x]
            first = jnp.where((lane >= 2 * x) & (lane < 2 * x + 2), turned, first)
            spot = (2 * x - 2) % N
            last = jnp.where((lane >= spot) & (lane < spot + 2), turned, last)
        shift = 2 * CELL * (i % 4)
        half = i // 4
        pack[0, half] = pack[0, half] + pltpu.roll(first, shift, 1)
        pack[1, half] = pack[1, half] + pltpu.roll(last, shift + 2, 1)

    loads[0].wait()

    def arrange(i, carry):
        block = jnp.swapaxes(fbuf[:, pl.ds(pl.multiple_of(i * CELL, CELL), CELL), :], 0, 1)
        xs[R, pl.ds(R + i * CELL, CELL)] = block
        total = block[0].astype(f32)
        for x in range(1, CELL):
            total = total + block[x].astype(f32)
        pooled[:, pl.ds(pl.multiple_of(i * N, N), N)] = total
        pack_edges(block, i, xpack)
        return carry

    lax.fori_loop(0, B, arrange, 0)

    def halo_copies(field, pack, right, left, send, recv):
        mid = field.at[R]
        plan = [
            (mid.at[pl.ds(R, R)], mid.at[pl.ds(R + N, R)], (-1, 0)),
            (mid.at[pl.ds(N, R)], mid.at[pl.ds(0, R)], (1, 0)),
            (pack.at[0], right.at[pl.ds(1, 2)], (0, -1)),
            (pack.at[1], left.at[pl.ds(1, 2)], (0, 1)),
            (pack.at[0, 0], right.at[3], (-1, -1)),
            (pack.at[0, 1], right.at[0], (1, -1)),
            (pack.at[1, 0], left.at[3], (-1, 1)),
            (pack.at[1, 1], left.at[0], (1, 1)),
        ]
        return [
            pltpu.make_async_remote_copy(
                src_ref=src, dst_ref=dst, send_sem=send.at[n], recv_sem=recv.at[n],
                device_id=at(*way), device_id_type=MESH,
            )
            for n, (src, dst, way) in enumerate(plan)
        ]

    def finish_halo(field, right, left):
        up, down = gx > 0, gx < nx - 1
        field[R, pl.ds(0, R)] = jnp.where(up, field[R, pl.ds(0, R)], jnp.zeros((R, C, N), bf16))
        field[R, pl.ds(R + N, R)] = jnp.where(
            down, field[R, pl.ds(R + N, R)], jnp.zeros((R, C, N), bf16)
        )
        for side, inside in ((right, gy < ny - 1), (left, gy > 0)):
            for part, there in ((0, inside & up), (1, inside), (2, inside), (3, inside & down)):
                side[part] = jnp.where(there, side[part], jnp.zeros((C, N), bf16))

        for part in range(4):
            for half in range(2):
                one, two = (left[part], pltpu.roll(right[part], C, 1))
                if half:
                    one, two = (pltpu.roll(left[part], C, 1), right[part])
                edges[2 * part + half] = jnp.where(low, one, two)

        def shift(step, carry):
            rows = []
            for n in range(SLABS):
                t = step * SLABS + n
                place = t + (C - R)
                turn = lax.rem(N - 2 * lax.rem(place, 32), N)
                rows.append(
                    jnp.concatenate([field[R, t], pltpu.roll(edges[place // 32], turn, 1)], axis=1)
                )
            moved = dot(jnp.concatenate(rows, axis=0), mover[...]).astype(bf16)
            for n, o in enumerate((0, 1, 3, 4)):
                field[o, pl.ds(step * SLABS, SLABS)] = moved[:, n * N : (n + 1) * N].reshape(
                    SLABS, C, N
                )
            return carry

        lax.fori_loop(0, HALO // SLABS, shift, 0)

    def around():
        return [(dx, dy) for dx in (-1, 0, 1) for dy in (-1, 0, 1) if (dx, dy) != (0, 0)]

    def line(axis, src, dst, send, recv):
        n = nx if axis == "gx" else ny
        me = gx if axis == "gx" else gy

        def copy(j, source, target):
            peer = lax.rem(me + j, n)
            return pltpu.make_async_remote_copy(
                src_ref=src(source(peer)), dst_ref=dst(target), send_sem=send.at[j],
                recv_sem=recv.at[j],
                device_id=(peer, gy) if axis == "gx" else (gx, peer), device_id_type=MESH,
            )

        def start():
            def step(j, carry):
                copy(j, lambda peer: peer, me).start()
                return carry

            lax.fori_loop(1, n, step, 0)

        def wait():
            def step(j, carry):
                copy(j, lambda peer: peer, lax.rem(me + n - j, n)).wait_recv()
                copy(j, lambda peer: peer, me).wait_send()
                return carry

            lax.fori_loop(1, n, step, 0)

        return start, wait

    pl.semaphore_wait(barrier, nx - 1 + ny - 1 + 4)
    xhalo = halo_copies(xs, xpack, xright, xleft, halo_s, halo_r)
    for copy in xhalo:
        copy.start()

    coarse = (split_dot(pooled[...], spread[...], NT) / CELL).astype(bf16)
    coarse_nb[4] = coarse
    ones = jnp.where(lax.broadcasted_iota(jnp.int32, (8, N), 1) < C, 1.0, 0.0)

    def as_row(values):
        sums = dot(ones, values, NT, HIGHEST)
        return jnp.concatenate([sums, jnp.zeros((8, N - C), f32)], axis=1)

    top1[gy] = as_row(coarse.astype(f32)) / B

    coarse_copies = []
    for n, (dx, dy) in enumerate(around()):
        slot = (1 - dx) * 3 + (1 - dy)
        copy = pltpu.make_async_remote_copy(
            src_ref=coarse_nb.at[4], dst_ref=coarse_nb.at[slot], send_sem=co_s.at[n],
            recv_sem=co_r.at[n], device_id=at(dx, dy), device_id_type=MESH,
        )
        copy.start()
        coarse_copies.append(copy)
    t1_start, t1_wait = line("gy", lambda p: top1.at[gy], lambda p: top1.at[p], t1_s, t1_r)
    t1_start()

    hpack[...] = jnp.zeros_like(hpack)
    source = lax.broadcasted_iota(jnp.int32, (2 * N, N), 0)
    for n, o in enumerate((0, 1, 3, 4)):
        y = lax.broadcasted_iota(jnp.int32, (2 * N, N), 1) + (o - R)
        y = jnp.where(y < 0, y + N + R, jnp.where(y >= N, y + C, y))
        mover[:, n * N : (n + 1) * N] = jnp.where(source == y, 1.0, 0.0).astype(bf16)
    def widen(k, carry):
        block = nw[k].astype(f32)
        wide[k] = jnp.concatenate([block, block], axis=1)
        turned = block.T
        wide_t[k] = jnp.concatenate([turned, turned], axis=1)
        return carry

    lax.fori_loop(0, K, widen, 0, unroll=4)

    code = (offs[pl.ds(0, 1), :] + R) * W + offs[pl.ds(1, 1), :] + R

    def coded(points, stride, first):
        row = lax.broadcasted_iota(jnp.int32, (points, K), 0) * stride + first
        col = lax.broadcasted_iota(jnp.int32, (points, K), 1)
        hit = jnp.where(row == col, jnp.broadcast_to(code, (points, K)).astype(f32), 0.0)
        own = jnp.sum(hit, axis=1, keepdims=True).astype(jnp.int32)
        return jnp.broadcast_to(own, (points, N))

    codes[...] = coded(K, 1, 0)

    def place(p, carry):
        plain = jnp.zeros((C, N), f32)
        turned = jnp.zeros((C, N), f32)
        for k in range(K):
            mine = codes[pl.ds(k, 1), :] == p
            plain = plain + jnp.where(mine, wide[k], 0.0)
            turned = turned + jnp.where(mine, wide_t[k], 0.0)
        w5[p] = plain.astype(bf16)
        w5t[p] = turned.astype(bf16)
        return carry

    lax.fori_loop(0, W * W, place, 0, unroll=5)
    nothing = jnp.zeros((C, N), bf16)

    def band(o, carry):
        for s in range(GROUP):
            for j in range(BAND // 2):
                ahead, back = [], []
                for r in (2 * j, 2 * j + 1):
                    a = r - s
                    inside = 0 <= a < W
                    ahead.append(w5t[a * W + o] if inside else nothing)
                    back.append(w5[(W - 1 - a) * W + (W - 1 - o)] if inside else nothing)
                cols = pl.ds(pl.multiple_of(o * BAND * C + j * N, N), N)
                fwd[pl.ds(s * C, C), cols] = jnp.where(low, ahead[0], ahead[1])
                bwd[pl.ds(s * C, C), cols] = jnp.where(low, back[0], back[1])
        return carry

    lax.fori_loop(0, W, band, 0, unroll=True)

    loads[2].wait()
    lane8 = lax.broadcasted_iota(jnp.int32, (L, N), 1)
    found = jnp.zeros((L, N), jnp.int32)
    for i in range(B):
        turned = pltpu.roll(abuf[i], lax.rem(N + i * B - gy * B, N), 1)
        found = jnp.where((lane8 >= i * B) & (lane8 < i * B + B), turned, found)
    rows = (found >> 7) - gx * B + B
    cols = (found & 127) - gy * B + B
    spot = ((rows >> 3) * 3 + (cols >> 3)) * C + (rows & 7) * B + (cols & 7)
    idx[...] = jnp.where(lane8 < C, spot, -1)

    def build_onehot(l, carry):
        target = lax.broadcasted_iota(jnp.int32, (TARGETS, N), 0)
        onehot[l] = jnp.where(target == idx[pl.ds(l, 1), :], 1.0, 0.0).astype(bf16)
        return carry

    lax.fori_loop(0, L, build_onehot, 0)

    t1_wait()
    top2[gx] = top1[:, 0, :]
    t2_start, t2_wait = line("gx", lambda p: top2.at[gx], lambda p: top2.at[p], t2_s, t2_r)
    t2_start()

    for copy in xhalo:
        copy.wait()
    finish_halo(xs, xright, xleft)

    for copy in coarse_copies:
        copy.wait()
    pieces = [
        jnp.where(low, coarse_nb[2 * j], coarse_nb[2 * j + 1] if j < 4 else nothing)
        for j in range(5)
    ]
    around_cells = jnp.concatenate(pieces, axis=1)

    def pick(l, total):
        chosen = dot(around_cells, onehot[l]).astype(bf16)
        picked[l] = chosen
        turned = lw[l].astype(f32).T.astype(bf16)
        return total + dot(turned, chosen)

    level_one = lax.fori_loop(0, L, pick, jnp.zeros((C, N), f32), unroll=True)
    def banded(matrix, field, pair):
        parts = []
        for o in range(W):
            first = field[o, pl.ds(pair * 8, BAND)].reshape(BAND * C, N)
            second = field[o, pl.ds(pair * 8 + GROUP, BAND)].reshape(BAND * C, N)
            parts.append(jnp.concatenate([first, second], axis=1))
        return dot(matrix[...], jnp.concatenate(parts, axis=0))

    def near_field(pair):
        near_buf[pair] = banded(fwd, xs, pair)

    for pair in range(B):
        near_field(pair)
    t2_wait()
    me = gx * ny + gy
    top_all = top2[...].reshape(N, N)
    tw_f32 = tw[...].astype(f32)
    mixed = dot(tw_f32.T, top_all[:, :C], NT, HIGHEST)
    level_two = jnp.sum(mixed * tk[pl.ds(me, 1), :], axis=1, keepdims=True)
    spread_one = split_dot(level_one[:, :C], spread[pl.ds(0, C), :]) + level_two
    for i in range(B):
        base[i] = spread_one[:, i * N : (i + 1) * N]

    loads[1].wait()

    def forward(i):
        rows16 = pl.ds(i * CELL, CELL)
        upstream = jnp.swapaxes(cbuf[:, rows16, :], 0, 1)
        shared = base[i]
        actives = []
        total = jnp.zeros((C, N), f32)
        for half in range(2):
            for g in range(2):
                for s in range(GROUP):
                    x = half * 8 + g * GROUP + s
                    near = near_buf[i * 2 + half, pl.ds(s * C, C), pl.ds(g * N, N)]
                    v = near + shared
                    square = v * v
                    tangent = jnp.tanh(v * (root_scale + root_scale * cubic_term * square))
                    gate = 0.5 + 0.5 * tangent
                    actives.append(v * gate)
                    slope = gate + v * (gate - gate * gate) * (
                        2.0 * root_scale + 6.0 * root_scale * cubic_term * square
                    )
                    grad = (upstream[x].astype(f32) * slope).astype(bf16)
                    hs[R, R + i * CELL + x] = grad
                    total = total + grad.astype(f32)
        pooled[:, pl.ds(i * N, N)] = total
        active = jnp.swapaxes(jnp.stack(actives), 0, 1)
        obuf[:, rows16, :] = (fbuf[:, rows16, :].astype(f32) + active).astype(bf16)

    def weigh(o, half):
        groups = [half * (N // GROUP // 2) + i for i in range(N // GROUP // 2)]
        left = jnp.concatenate(
            [xs[o, pl.ds(i * GROUP, BAND)].reshape(BAND * C, N) for i in groups], axis=1
        )
        right = jnp.concatenate(
            [hs[R, pl.ds(R + i * GROUP, GROUP)].reshape(GROUP * C, N) for i in groups], axis=1
        )
        return dot(left, right, NT)

    for i in range(B // 2):
        near_field(B + 2 * i)
        near_field(B + 2 * i + 1)
        forward(i)
    for i in range(B // 2):
        grads[i] = weigh(i, 0)
        forward(B // 2 + i)

    one = split_dot(pooled[...], spread[...], NT)
    one_ref[...] = one
    two1[gy] = as_row(one)
    u1_start, u1_wait = line("gy", lambda p: two1.at[gy], lambda p: two1.at[p], u1_s, u1_r)
    u1_start()

    for o in range(W):
        grads[o] = weigh(o, 1) + (grads[o] if o < B // 2 else weigh(o, 0))
    u1_wait()
    two2[gx] = two1[:, 0, :]
    u2_start, u2_wait = line("gx", lambda p: two2.at[gx], lambda p: two2.at[p], u2_s, u2_r)
    u2_start()

    def stencil_grad(p, carry):
        a = p // W
        b = lax.rem(p, W)
        part = [
            grads[b, pl.ds(pl.multiple_of((a + s) * C, C), C), pl.ds((s // 2) * N, N)]
            for s in range(GROUP)
        ]
        both = jnp.where(low, part[0] + part[2], part[1] + part[3])
        both = both + pltpu.roll(both, C, 1)
        stencil[p] = jnp.where(low[:32], both[:32], both[32:])
        return carry

    lax.fori_loop(0, W * W, stencil_grad, 0, unroll=True)

    for k in range(K):
        rs_src[k, pl.ds(0, 32), :] = stencil[(spots[0, k] + R) * W + spots[1, k] + R].astype(bf16)

    def link_grads(l, carry):
        grad = dot_split(picked[l], one_ref[...], NT)
        for half in range(2):
            rows = [grad[(2 * half + n) * 16 : (2 * half + n + 1) * 16] for n in range(2)]
            rs_src[2 * l + half, pl.ds(32, 16), :] = jnp.concatenate(
                [rows[0][:, :C], rows[1][:, :C]], axis=1
            ).astype(bf16)
        return carry

    lax.fori_loop(0, L, link_grads, 0, unroll=True)
    rs1[gy] = rs_src[gy]
    r1_start, r1_wait = line("gy", lambda p: rs_src.at[p], lambda p: rs1.at[p], r1_s, r1_r)
    r1_start()

    def pack_hidden(i, carry):
        pack_edges(hs[R, pl.ds(R + i * CELL, CELL)], i, hpack)
        return carry

    lax.fori_loop(0, B, pack_hidden, 0)
    hhalo = halo_copies(hs, hpack, hright, hleft, hhalo_s, hhalo_r)
    for copy in hhalo:
        copy.start()

    def push(l, total):
        grad = one_ref[...]
        pushed = dot_split(lw[l], grad)
        return total + split_dot(pushed, onehot[l], NT, 2)

    pushes = lax.fori_loop(0, L, push, jnp.zeros((C, TARGETS), f32), unroll=True)
    for j in range(5):
        ctr[j] = pushes[:, j * N : (j + 1) * N]
    push_copies = []
    for n, (dx, dy) in enumerate(around()):
        slot = (1 - dx) * 3 + (1 - dy)
        copy = pltpu.make_async_remote_copy(
            src_ref=ctr.at[(8 - slot) // 2], dst_ref=rctr.at[slot], send_sem=ct_s.at[n],
            recv_sem=ct_r.at[n], device_id=at(dx, dy), device_id_type=MESH,
        )
        copy.start()
        push_copies.append(copy)

    r1_wait()
    total = rs1[0].astype(f32)
    for j in range(1, ny):
        total = total + rs1[j].astype(f32)
    rs2[gx] = total.astype(bf16)
    r2_start, r2_wait = line("gx", lambda p: rs2.at[gx], lambda p: rs2.at[p], r2_s, r2_r)
    r2_start()

    for copy in hhalo:
        copy.wait()
    finish_halo(hs, hright, hleft)

    for copy in push_copies:
        copy.wait()
    evens = ctr[2]
    odds = jnp.zeros((C, N), f32)
    for slot in range(9):
        if slot == 4:
            continue
        if slot % 2 == 0:
            evens = evens + rctr[slot]
        else:
            odds = odds + rctr[slot]
    collected = evens + pltpu.roll(odds, C, 1)
    u2_wait()
    two_all = two2[...].reshape(N, N)[:, :C]
    kernel_grad = dot(tk[...], two_all, TN, HIGHEST)
    top_all = top2[...].reshape(N, N)
    top_out[...] = dot(top_all[:, :C], kernel_grad, TN, HIGHEST)
    mine = lax.broadcasted_iota(jnp.int32, (N, C), 0) == me
    kernel_row = jnp.sum(jnp.where(mine, kernel_grad, 0.0), axis=0, keepdims=True)
    top_coef_grad = jnp.sum(tw[...].astype(f32) * kernel_row, axis=1, keepdims=True)
    coarse_grad = (collected + top_coef_grad / B) / CELL
    spread_grad = split_dot(coarse_grad[:, :C], spread[pl.ds(0, C), :])
    for i in range(B):
        base[i] = spread_grad[:, i * N : (i + 1) * N]

    def backward(i, carry):
        rows16 = pl.ds(pl.multiple_of(i * CELL, CELL), CELL)
        shared = base[i]
        sums = []
        for half in range(2):
            near = banded(bwd, hs, i * 2 + half)
            for g in range(2):
                for s in range(GROUP):
                    sums.append(near[s * C : (s + 1) * C, g * N : (g + 1) * N] + shared)
        total = jnp.swapaxes(jnp.stack(sums), 0, 1)
        ibuf[:, rows16, :] = (cbuf[:, rows16, :].astype(f32) + total).astype(bf16)
        return carry

    lax.fori_loop(0, 1, backward, 0, unroll=True)
    r2_wait()
    total = rs2[0].astype(f32)
    for j in range(1, nx):
        total = total + rs2[j].astype(f32)
    ag[gy] = total.astype(bf16)
    a1_start, a1_wait = line("gy", lambda p: ag.at[gy], lambda p: ag.at[p], a1_s, a1_r)
    a1_start()
    lax.fori_loop(1, B, backward, 0, unroll=True)
    a1_wait()
    for k in range(K):
        whole = ag[k].astype(f32)
        near_out[k, pl.ds(0, 32), :] = whole[:32, :C]
        near_out[k, pl.ds(32, 32), :] = pltpu.roll(whole[:32], C, 1)[:, :C]
        link_out[k // 2, pl.ds((k % 2) * 32, 16), :] = whole[32:, :C]
        link_out[k // 2, pl.ds((k % 2) * 32 + 16, 16), :] = pltpu.roll(whole[32:], C, 1)[:, :C]


def store(*refs):
    count = len(refs) // 2
    sems = refs[-1]
    copies = [
        pltpu.make_async_copy(refs[n], refs[count + n], sems.at[n]) for n in range(count)
    ]
    for copy in copies:
        copy.start()
    for copy in copies:
        copy.wait()


def solution(mesh):
    nx, ny = mesh.shape["gx"], mesh.shape["gy"]
    vmem = pl.BlockSpec(memory_space=pltpu.VMEM)
    anywhere = pl.BlockSpec(memory_space=pl.ANY)
    dma = pltpu.SemaphoreType.DMA

    def per_device(feat, cot, offsets, adjacency, near_w, link_w, top_w, top_k):
        scratch = [
            pltpu.VMEM((C, N, N), bf16),
            pltpu.VMEM((C, N, N), bf16),
            pltpu.VMEM((B, L, N), jnp.int32),
            pltpu.VMEM((W, HALO, C, N), bf16),
            pltpu.VMEM((W, HALO, C, N), bf16),
            pltpu.VMEM((2, 2, C, N), bf16),
            pltpu.VMEM((2, 2, C, N), bf16),
            pltpu.VMEM((4, C, N), bf16),
            pltpu.VMEM((4, C, N), bf16),
            pltpu.VMEM((4, C, N), bf16),
            pltpu.VMEM((4, C, N), bf16),
            pltpu.VMEM((K, C, N), f32),
            pltpu.VMEM((K, C, N), f32),
            pltpu.VMEM((W * W, C, N), bf16),
            pltpu.VMEM((W * W, C, N), bf16),
            pltpu.VMEM((GROUP * C, W * BAND * C), bf16),
            pltpu.VMEM((GROUP * C, W * BAND * C), bf16),
            pltpu.VMEM((N, B * N), bf16),
            pltpu.VMEM((C, B * N), f32),
            pltpu.VMEM((L, TARGETS, N), bf16),
            pltpu.VMEM((L, N), jnp.int32),
            pltpu.VMEM((9, C, N), bf16),
            pltpu.VMEM((L, C, N), bf16),
            pltpu.VMEM((B, C, N), f32),
            pltpu.VMEM((ny, 8, N), f32),
            pltpu.VMEM((nx, ny, N), f32),
            pltpu.VMEM((ny, 8, N), f32),
            pltpu.VMEM((nx, ny, N), f32),
            pltpu.VMEM((5, C, N), f32),
            pltpu.VMEM((9, C, N), f32),
            pltpu.VMEM((W, BAND * C, GROUP * C), f32),
            pltpu.VMEM((ny, 48, N), bf16),
            pltpu.VMEM((ny, 48, N), bf16),
            pltpu.VMEM((nx, 48, N), bf16),
            pltpu.VMEM((ny, 48, N), bf16),
            pltpu.VMEM((C, N), f32),
            pltpu.VMEM((K, N), jnp.int32),
            pltpu.VMEM((2 * N, 4 * N), bf16),
            pltpu.VMEM((8, C, N), bf16),
            pltpu.VMEM((N // (2 * GROUP), GROUP * C, 2 * N), f32),
            pltpu.VMEM((W * W, 32, N), f32),
            dma((3,)),
            dma((8,)), dma((8,)), dma((8,)), dma((8,)),
            dma((8,)), dma((8,)), dma((8,)), dma((8,)),
            dma((ny,)), dma((ny,)), dma((nx,)), dma((nx,)),
            dma((ny,)), dma((ny,)), dma((nx,)), dma((nx,)),
            dma((ny,)), dma((ny,)), dma((nx,)), dma((nx,)), dma((ny,)), dma((ny,)),
        ]
        results = (
            ((C, N, N), bf16),
            ((C, N, N), bf16),
            ((K, C, C), f32),
            ((L, C, C), f32),
            ((C, C), f32),
        )
        held = pl.pallas_call(
            functools.partial(kernel, nx, ny),
            out_shape=[pltpu.VMEM(*result) for result in results],
            in_specs=[
                anywhere, anywhere, anywhere,
                vmem,
                pl.BlockSpec(memory_space=pltpu.SMEM),
                vmem, vmem, vmem, vmem,
            ],
            out_specs=[vmem] * 5,
            scratch_shapes=scratch,
            compiler_params=pltpu.CompilerParams(
                collective_id=0, has_side_effects=True, vmem_limit_bytes=54 * 2**20
            ),
        )(
            feat, cot, jnp.transpose(adjacency, (0, 2, 1)), offsets.T, offsets.T, near_w, link_w,
            top_w, top_k,
        )
        return pl.pallas_call(
            store,
            out_shape=[jax.ShapeDtypeStruct(*result) for result in results],
            in_specs=[vmem] * 5,
            out_specs=[anywhere] * 5,
            scratch_shapes=[dma((5,))],
            compiler_params=pltpu.CompilerParams(vmem_limit_bytes=2**20),
        )(*[pltpu.with_memory_space_constraint(value, pltpu.VMEM) for value in held])

    return jax.shard_map(
        per_device,
        mesh=mesh,
        in_specs=(P(None, "gx", "gy"), P(None, "gx", "gy"), P(), P(), P(), P(), P(), P()),
        out_specs=(P(None, "gx", "gy"), P(None, "gx", "gy"), P(), P(), P()),
        check_vma=False,
    )
```

```python
import functools

import jax
import jax.numpy as jnp
from jax import lax
from jax.experimental import pallas as pl
from jax.experimental.pallas import tpu as pltpu
from jax.sharding import PartitionSpec as P

C = 64
N = 128
K = 16
L = 8
CELL = 16
B = 8
W = 5
R = 2
HALO = N + 2 * R
GROUP = 4
BAND = GROUP + 2 * R
SLABS = 66
TARGETS = 640

root_scale = 0.7978845608028654
cubic_term = 0.044715

bf16 = jnp.bfloat16
f32 = jnp.float32
MESH = pl.DeviceIdType.MESH
HIGHEST = lax.Precision.HIGHEST
NT = (((1,), (1,)), ((), ()))
NN = (((1,), (0,)), ((), ()))
TN = (((0,), (0,)), ((), ()))


def dot(a, b, dims=NN, precision=None):
    return lax.dot_general(a, b, dims, preferred_element_type=f32, precision=precision)


def split_dot(a, b, dims=NN, terms=3):
    total = None
    for _ in range(terms):
        high = a.astype(bf16)
        part = dot(high, b, dims)
        total = part if total is None else total + part
        a = a - high.astype(f32)
    return total


def dot_split(a, b, dims=NN, terms=2):
    total = None
    for _ in range(terms):
        high = b.astype(bf16)
        part = dot(a, high, dims)
        total = part if total is None else total + part
        b = b - high.astype(f32)
    return total


def kernel(
    nx, ny,
    feat, cot, adj, offs_in, spots, nw_in, lw_in, tw_in, tk_in,
    obuf, ibuf, near_out, link_out, top_out,
    fbuf, cbuf, abuf, offs, nw, lw, tw, tk, xs, hs, xpack, hpack, xright, xleft, hright, hleft,
    wide, wide_t, w5, w5t, fwd, bwd, spread, pooled, onehot, idx,
    coarse_nb, picked, base, top1, top2, two1, two2, ctr, rctr, grads,
    rs_src, rs1, rs2, ag, one_ref, codes, mover, edges, near_buf, stencil,
    load_sem, halo_s, halo_r, hhalo_s, hhalo_r, co_s, co_r, ct_s, ct_r,
    t1_s, t1_r, t2_s, t2_r, u1_s, u1_r, u2_s, u2_r,
    r1_s, r1_r, r2_s, r2_r, a1_s, a1_r,
):
    gx = lax.axis_index("gx")
    gy = lax.axis_index("gy")

    def at(dx, dy):
        return (lax.rem(gx + dx + nx, nx), lax.rem(gy + dy + ny, ny))

    quarter = N // 4
    field_loads = [
        pltpu.make_async_copy(
            feat.at[:, pl.ds(n * quarter, quarter), :], fbuf.at[:, pl.ds(n * quarter, quarter), :],
            load_sem.at[n],
        )
        for n in range(4)
    ]
    loads = field_loads + [
        pltpu.make_async_copy(source, target, load_sem.at[4 + n])
        for n, (source, target) in enumerate(
            (
                (offs_in, offs), (nw_in, nw), (adj.at[pl.ds(gx * B, B)], abuf), (lw_in, lw),
                (tw_in, tw), (tk_in, tk), (cot, cbuf),
            )
        )
    ]
    for load in loads:
        load.start()

    barrier = pltpu.get_barrier_semaphore()
    for j in range(1, nx):
        pl.semaphore_signal(barrier, inc=1, device_id=at(j, 0), device_id_type=MESH)
    for j in range(1, ny):
        pl.semaphore_signal(barrier, inc=1, device_id=at(0, j), device_id_type=MESH)
    for dx in (-1, 1):
        for dy in (-1, 1):
            pl.semaphore_signal(barrier, inc=1, device_id=at(dx, dy), device_id_type=MESH)

    lane = lax.broadcasted_iota(jnp.int32, (C, N), 1)
    low = lane < C

    def build_spread(i, carry):
        rows = lax.broadcasted_iota(jnp.int32, (N, N), 0) % C
        cols = lax.broadcasted_iota(jnp.int32, (N, N), 1) // CELL + i * B
        hit = jnp.where(rows == cols, 1.0, 0.0).astype(bf16)
        spread[:, pl.ds(pl.multiple_of(i * N, N), N)] = hit
        return carry

    lax.fori_loop(0, B, build_spread, 0)
    xpack[...] = jnp.zeros_like(xpack)

    def pack_edges(block, i, pack):
        first = jnp.zeros((C, N), bf16)
        last = jnp.zeros((C, N), bf16)
        for x in range(CELL):
            turned = pltpu.roll(block[x], 2 * x, 1) if x else block[x]
            first = jnp.where((lane >= 2 * x) & (lane < 2 * x + 2), turned, first)
            spot = (2 * x - 2) % N
            last = jnp.where((lane >= spot) & (lane < spot + 2), turned, last)
        shift = 2 * CELL * (i % 4)
        half = i // 4
        pack[0, half] = pack[0, half] + pltpu.roll(first, shift, 1)
        pack[1, half] = pack[1, half] + pltpu.roll(last, shift + 2, 1)


    def arrange(i, carry):
        block = jnp.swapaxes(fbuf[:, pl.ds(pl.multiple_of(i * CELL, CELL), CELL), :], 0, 1)
        xs[R, pl.ds(R + i * CELL, CELL)] = block
        total = block[0].astype(f32)
        for x in range(1, CELL):
            total = total + block[x].astype(f32)
        pooled[:, pl.ds(pl.multiple_of(i * N, N), N)] = total
        pack_edges(block, i, xpack)
        return carry

    for n in range(4):
        field_loads[n].wait()
        lax.fori_loop(2 * n, 2 * n + 2, arrange, 0)

    def halo_copies(field, pack, right, left, send, recv):
        mid = field.at[R]
        plan = [
            (mid.at[pl.ds(R, R)], mid.at[pl.ds(R + N, R)], (-1, 0)),
            (mid.at[pl.ds(N, R)], mid.at[pl.ds(0, R)], (1, 0)),
            (pack.at[0], right.at[pl.ds(1, 2)], (0, -1)),
            (pack.at[1], left.at[pl.ds(1, 2)], (0, 1)),
            (pack.at[0, 0], right.at[3], (-1, -1)),
            (pack.at[0, 1], right.at[0], (1, -1)),
            (pack.at[1, 0], left.at[3], (-1, 1)),
            (pack.at[1, 1], left.at[0], (1, 1)),
        ]
        return [
            pltpu.make_async_remote_copy(
                src_ref=src, dst_ref=dst, send_sem=send.at[n], recv_sem=recv.at[n],
                device_id=at(*way), device_id_type=MESH,
            )
            for n, (src, dst, way) in enumerate(plan)
        ]

    def finish_halo(field, right, left):
        up, down = gx > 0, gx < nx - 1
        field[R, pl.ds(0, R)] = jnp.where(up, field[R, pl.ds(0, R)], jnp.zeros((R, C, N), bf16))
        field[R, pl.ds(R + N, R)] = jnp.where(
            down, field[R, pl.ds(R + N, R)], jnp.zeros((R, C, N), bf16)
        )
        for side, inside in ((right, gy < ny - 1), (left, gy > 0)):
            for part, there in ((0, inside & up), (1, inside), (2, inside), (3, inside & down)):
                side[part] = jnp.where(there, side[part], jnp.zeros((C, N), bf16))

        for part in range(4):
            for half in range(2):
                one, two = (left[part], pltpu.roll(right[part], C, 1))
                if half:
                    one, two = (pltpu.roll(left[part], C, 1), right[part])
                edges[2 * part + half] = jnp.where(low, one, two)

        def shift(step, carry):
            rows = []
            for n in range(SLABS):
                t = step * SLABS + n
                place = t + (C - R)
                turn = lax.rem(N - 2 * lax.rem(place, 32), N)
                rows.append(
                    jnp.concatenate([field[R, t], pltpu.roll(edges[place // 32], turn, 1)], axis=1)
                )
            moved = dot(jnp.concatenate(rows, axis=0), mover[...]).astype(bf16)
            for n, o in enumerate((0, 1, 3, 4)):
                field[o, pl.ds(step * SLABS, SLABS)] = moved[:, n * N : (n + 1) * N].reshape(
                    SLABS, C, N
                )
            return carry

        lax.fori_loop(0, HALO // SLABS, shift, 0)

    def around():
        return [(dx, dy) for dx in (-1, 0, 1) for dy in (-1, 0, 1) if (dx, dy) != (0, 0)]

    def line(axis, src, dst, send, recv):
        n = nx if axis == "gx" else ny
        me = gx if axis == "gx" else gy

        def copy(j, source, target):
            peer = lax.rem(me + j, n)
            return pltpu.make_async_remote_copy(
                src_ref=src(source(peer)), dst_ref=dst(target), send_sem=send.at[j],
                recv_sem=recv.at[j],
                device_id=(peer, gy) if axis == "gx" else (gx, peer), device_id_type=MESH,
            )

        def start():
            def step(j, carry):
                copy(j, lambda peer: peer, me).start()
                return carry

            lax.fori_loop(1, n, step, 0)

        def wait():
            def step(j, carry):
                copy(j, lambda peer: peer, lax.rem(me + n - j, n)).wait_recv()
                copy(j, lambda peer: peer, me).wait_send()
                return carry

            lax.fori_loop(1, n, step, 0)

        return start, wait

    pl.semaphore_wait(barrier, nx - 1 + ny - 1 + 4)
    xhalo = halo_copies(xs, xpack, xright, xleft, halo_s, halo_r)
    for copy in xhalo:
        copy.start()

    coarse = (split_dot(pooled[...], spread[...], NT) / CELL).astype(bf16)
    coarse_nb[4] = coarse
    ones = jnp.where(lax.broadcasted_iota(jnp.int32, (8, N), 1) < C, 1.0, 0.0)

    def as_row(values):
        sums = dot(ones, values, NT, HIGHEST)
        return jnp.concatenate([sums, jnp.zeros((8, N - C), f32)], axis=1)

    top1[gy] = as_row(coarse.astype(f32)) / B

    coarse_copies = []
    for n, (dx, dy) in enumerate(around()):
        slot = (1 - dx) * 3 + (1 - dy)
        copy = pltpu.make_async_remote_copy(
            src_ref=coarse_nb.at[4], dst_ref=coarse_nb.at[slot], send_sem=co_s.at[n],
            recv_sem=co_r.at[n], device_id=at(dx, dy), device_id_type=MESH,
        )
        copy.start()
        coarse_copies.append(copy)
    t1_start, t1_wait = line("gy", lambda p: top1.at[gy], lambda p: top1.at[p], t1_s, t1_r)
    t1_start()

    hpack[...] = jnp.zeros_like(hpack)
    source = lax.broadcasted_iota(jnp.int32, (2 * N, N), 0)
    for n, o in enumerate((0, 1, 3, 4)):
        y = lax.broadcasted_iota(jnp.int32, (2 * N, N), 1) + (o - R)
        y = jnp.where(y < 0, y + N + R, jnp.where(y >= N, y + C, y))
        mover[:, n * N : (n + 1) * N] = jnp.where(source == y, 1.0, 0.0).astype(bf16)
    for load in loads[4:]:
        load.wait()
    def widen(k, carry):
        block = nw[k].astype(f32)
        wide[k] = jnp.concatenate([block, block], axis=1)
        turned = block.T
        wide_t[k] = jnp.concatenate([turned, turned], axis=1)
        return carry

    lax.fori_loop(0, K, widen, 0, unroll=4)

    code = (offs[pl.ds(0, 1), :] + R) * W + offs[pl.ds(1, 1), :] + R

    def coded(points, stride, first):
        row = lax.broadcasted_iota(jnp.int32, (points, K), 0) * stride + first
        col = lax.broadcasted_iota(jnp.int32, (points, K), 1)
        hit = jnp.where(row == col, jnp.broadcast_to(code, (points, K)).astype(f32), 0.0)
        own = jnp.sum(hit, axis=1, keepdims=True).astype(jnp.int32)
        return jnp.broadcast_to(own, (points, N))

    codes[...] = coded(K, 1, 0)

    def place(p, carry):
        plain = jnp.zeros((C, N), f32)
        turned = jnp.zeros((C, N), f32)
        for k in range(K):
            mine = codes[pl.ds(k, 1), :] == p
            plain = plain + jnp.where(mine, wide[k], 0.0)
            turned = turned + jnp.where(mine, wide_t[k], 0.0)
        w5[p] = plain.astype(bf16)
        w5t[p] = turned.astype(bf16)
        return carry

    lax.fori_loop(0, W * W, place, 0, unroll=5)
    nothing = jnp.zeros((C, N), bf16)

    def band(o, carry):
        for s in range(GROUP):
            for j in range(BAND // 2):
                ahead, back = [], []
                for r in (2 * j, 2 * j + 1):
                    a = r - s
                    inside = 0 <= a < W
                    ahead.append(w5t[a * W + o] if inside else nothing)
                    back.append(w5[(W - 1 - a) * W + (W - 1 - o)] if inside else nothing)
                cols = pl.ds(pl.multiple_of(o * BAND * C + j * N, N), N)
                fwd[pl.ds(s * C, C), cols] = jnp.where(low, ahead[0], ahead[1])
                bwd[pl.ds(s * C, C), cols] = jnp.where(low, back[0], back[1])
        return carry

    lax.fori_loop(0, W, band, 0, unroll=True)

    lane8 = lax.broadcasted_iota(jnp.int32, (L, N), 1)
    found = jnp.zeros((L, N), jnp.int32)
    for i in range(B):
        turned = pltpu.roll(abuf[i], lax.rem(N + i * B - gy * B, N), 1)
        found = jnp.where((lane8 >= i * B) & (lane8 < i * B + B), turned, found)
    rows = (found >> 7) - gx * B + B
    cols = (found & 127) - gy * B + B
    spot = ((rows >> 3) * 3 + (cols >> 3)) * C + (rows & 7) * B + (cols & 7)
    idx[...] = jnp.where(lane8 < C, spot, -1)

    def build_onehot(l, carry):
        target = lax.broadcasted_iota(jnp.int32, (TARGETS, N), 0)
        onehot[l] = jnp.where(target == idx[pl.ds(l, 1), :], 1.0, 0.0).astype(bf16)
        return carry

    lax.fori_loop(0, L, build_onehot, 0)

    t1_wait()
    top2[gx] = top1[:, 0, :]
    t2_start, t2_wait = line("gx", lambda p: top2.at[gx], lambda p: top2.at[p], t2_s, t2_r)
    t2_start()

    for copy in xhalo:
        copy.wait()
    finish_halo(xs, xright, xleft)

    for copy in coarse_copies:
        copy.wait()
    pieces = [
        jnp.where(low, coarse_nb[2 * j], coarse_nb[2 * j + 1] if j < 4 else nothing)
        for j in range(5)
    ]
    around_cells = jnp.concatenate(pieces, axis=1)

    def pick(l, total):
        chosen = dot(around_cells, onehot[l]).astype(bf16)
        picked[l] = chosen
        turned = lw[l].astype(f32).T.astype(bf16)
        return total + dot(turned, chosen)

    level_one = lax.fori_loop(0, L, pick, jnp.zeros((C, N), f32), unroll=True)
    def banded(matrix, field, pair):
        parts = []
        for o in range(W):
            first = field[o, pl.ds(pair * 8, BAND)].reshape(BAND * C, N)
            second = field[o, pl.ds(pair * 8 + GROUP, BAND)].reshape(BAND * C, N)
            parts.append(jnp.concatenate([first, second], axis=1))
        return dot(matrix[...], jnp.concatenate(parts, axis=0))

    def near_field(pair):
        near_buf[pair] = banded(fwd, xs, pair)

    for pair in range(B):
        near_field(pair)
    t2_wait()
    me = gx * ny + gy
    top_all = top2[...].reshape(N, N)
    tw_f32 = tw[...].astype(f32)
    mixed = dot(tw_f32.T, top_all[:, :C], NT, HIGHEST)
    level_two = jnp.sum(mixed * tk[pl.ds(me, 1), :], axis=1, keepdims=True)
    spread_one = split_dot(level_one[:, :C], spread[pl.ds(0, C), :]) + level_two
    for i in range(B):
        base[i] = spread_one[:, i * N : (i + 1) * N]


    def forward(i):
        rows16 = pl.ds(i * CELL, CELL)
        upstream = jnp.swapaxes(cbuf[:, rows16, :], 0, 1)
        shared = base[i]
        actives = []
        total = jnp.zeros((C, N), f32)
        for half in range(2):
            for g in range(2):
                for s in range(GROUP):
                    x = half * 8 + g * GROUP + s
                    near = near_buf[i * 2 + half, pl.ds(s * C, C), pl.ds(g * N, N)]
                    v = near + shared
                    square = v * v
                    tangent = jnp.tanh(v * (root_scale + root_scale * cubic_term * square))
                    gate = 0.5 + 0.5 * tangent
                    actives.append(v * gate)
                    slope = gate + v * (gate - gate * gate) * (
                        2.0 * root_scale + 6.0 * root_scale * cubic_term * square
                    )
                    grad = (upstream[x].astype(f32) * slope).astype(bf16)
                    hs[R, R + i * CELL + x] = grad
                    total = total + grad.astype(f32)
        pooled[:, pl.ds(i * N, N)] = total
        active = jnp.swapaxes(jnp.stack(actives), 0, 1)
        obuf[:, rows16, :] = (fbuf[:, rows16, :].astype(f32) + active).astype(bf16)

    def weigh(o, half):
        groups = [half * (N // GROUP // 2) + i for i in range(N // GROUP // 2)]
        left = jnp.concatenate(
            [xs[o, pl.ds(i * GROUP, BAND)].reshape(BAND * C, N) for i in groups], axis=1
        )
        right = jnp.concatenate(
            [hs[R, pl.ds(R + i * GROUP, GROUP)].reshape(GROUP * C, N) for i in groups], axis=1
        )
        return dot(left, right, NT)

    for i in range(B // 2):
        near_field(B + 2 * i)
        near_field(B + 2 * i + 1)
        forward(i)
    for i in range(B // 2):
        grads[i] = weigh(i, 0)
        forward(B // 2 + i)

    one = split_dot(pooled[...], spread[...], NT)
    one_ref[...] = one
    two1[gy] = as_row(one)
    u1_start, u1_wait = line("gy", lambda p: two1.at[gy], lambda p: two1.at[p], u1_s, u1_r)
    u1_start()

    for o in range(W):
        grads[o] = weigh(o, 1) + (grads[o] if o < B // 2 else weigh(o, 0))
    u1_wait()
    two2[gx] = two1[:, 0, :]
    u2_start, u2_wait = line("gx", lambda p: two2.at[gx], lambda p: two2.at[p], u2_s, u2_r)
    u2_start()

    def stencil_grad(p, carry):
        a = p // W
        b = lax.rem(p, W)
        part = [
            grads[b, pl.ds(pl.multiple_of((a + s) * C, C), C), pl.ds((s // 2) * N, N)]
            for s in range(GROUP)
        ]
        both = jnp.where(low, part[0] + part[2], part[1] + part[3])
        both = both + pltpu.roll(both, C, 1)
        stencil[p] = jnp.where(low[:32], both[:32], both[32:])
        return carry

    lax.fori_loop(0, W * W, stencil_grad, 0, unroll=True)

    for k in range(K):
        rs_src[k, pl.ds(0, 32), :] = stencil[(spots[0, k] + R) * W + spots[1, k] + R].astype(bf16)

    def link_grads(l, carry):
        grad = dot_split(picked[l], one_ref[...], NT)
        for half in range(2):
            rows = [grad[(2 * half + n) * 16 : (2 * half + n + 1) * 16] for n in range(2)]
            rs_src[2 * l + half, pl.ds(32, 16), :] = jnp.concatenate(
                [rows[0][:, :C], rows[1][:, :C]], axis=1
            ).astype(bf16)
        return carry

    lax.fori_loop(0, L, link_grads, 0, unroll=True)
    rs1[gy] = rs_src[gy]
    r1_start, r1_wait = line("gy", lambda p: rs_src.at[p], lambda p: rs1.at[p], r1_s, r1_r)
    r1_start()

    def pack_hidden(i, carry):
        pack_edges(hs[R, pl.ds(R + i * CELL, CELL)], i, hpack)
        return carry

    lax.fori_loop(0, B, pack_hidden, 0)
    hhalo = halo_copies(hs, hpack, hright, hleft, hhalo_s, hhalo_r)
    for copy in hhalo:
        copy.start()

    def push(l, total):
        grad = one_ref[...]
        pushed = dot_split(lw[l], grad)
        return total + split_dot(pushed, onehot[l], NT, 2)

    pushes = lax.fori_loop(0, L, push, jnp.zeros((C, TARGETS), f32), unroll=True)
    for j in range(5):
        ctr[j] = pushes[:, j * N : (j + 1) * N]
    push_copies = []
    for n, (dx, dy) in enumerate(around()):
        slot = (1 - dx) * 3 + (1 - dy)
        copy = pltpu.make_async_remote_copy(
            src_ref=ctr.at[(8 - slot) // 2], dst_ref=rctr.at[slot], send_sem=ct_s.at[n],
            recv_sem=ct_r.at[n], device_id=at(dx, dy), device_id_type=MESH,
        )
        copy.start()
        push_copies.append(copy)

    r1_wait()
    total = rs1[0].astype(f32)
    for j in range(1, ny):
        total = total + rs1[j].astype(f32)
    rs2[gx] = total.astype(bf16)
    r2_start, r2_wait = line("gx", lambda p: rs2.at[gx], lambda p: rs2.at[p], r2_s, r2_r)
    r2_start()

    for copy in hhalo:
        copy.wait()
    finish_halo(hs, hright, hleft)

    for copy in push_copies:
        copy.wait()
    evens = ctr[2]
    odds = jnp.zeros((C, N), f32)
    for slot in range(9):
        if slot == 4:
            continue
        if slot % 2 == 0:
            evens = evens + rctr[slot]
        else:
            odds = odds + rctr[slot]
    collected = evens + pltpu.roll(odds, C, 1)
    u2_wait()
    two_all = two2[...].reshape(N, N)[:, :C]
    kernel_grad = dot(tk[...], two_all, TN, HIGHEST)
    top_all = top2[...].reshape(N, N)
    top_out[...] = dot(top_all[:, :C], kernel_grad, TN, HIGHEST)
    mine = lax.broadcasted_iota(jnp.int32, (N, C), 0) == me
    kernel_row = jnp.sum(jnp.where(mine, kernel_grad, 0.0), axis=0, keepdims=True)
    top_coef_grad = jnp.sum(tw[...].astype(f32) * kernel_row, axis=1, keepdims=True)
    coarse_grad = (collected + top_coef_grad / B) / CELL
    spread_grad = split_dot(coarse_grad[:, :C], spread[pl.ds(0, C), :])
    for i in range(B):
        base[i] = spread_grad[:, i * N : (i + 1) * N]

    def backward(i, carry):
        rows16 = pl.ds(pl.multiple_of(i * CELL, CELL), CELL)
        shared = base[i]
        sums = []
        for half in range(2):
            near = banded(bwd, hs, i * 2 + half)
            for g in range(2):
                for s in range(GROUP):
                    sums.append(near[s * C : (s + 1) * C, g * N : (g + 1) * N] + shared)
        total = jnp.swapaxes(jnp.stack(sums), 0, 1)
        ibuf[:, rows16, :] = (cbuf[:, rows16, :].astype(f32) + total).astype(bf16)
        return carry

    lax.fori_loop(0, 1, backward, 0, unroll=True)
    r2_wait()
    total = rs2[0].astype(f32)
    for j in range(1, nx):
        total = total + rs2[j].astype(f32)
    ag[gy] = total.astype(bf16)
    a1_start, a1_wait = line("gy", lambda p: ag.at[gy], lambda p: ag.at[p], a1_s, a1_r)
    a1_start()
    lax.fori_loop(1, B, backward, 0, unroll=True)
    a1_wait()
    for k in range(K):
        whole = ag[k].astype(f32)
        near_out[k, pl.ds(0, 32), :] = whole[:32, :C]
        near_out[k, pl.ds(32, 32), :] = pltpu.roll(whole[:32], C, 1)[:, :C]
        link_out[k // 2, pl.ds((k % 2) * 32, 16), :] = whole[32:, :C]
        link_out[k // 2, pl.ds((k % 2) * 32 + 16, 16), :] = pltpu.roll(whole[32:], C, 1)[:, :C]


def store(*refs):
    count = len(refs) // 2
    sems = refs[-1]
    copies = []
    for n in range(count):
        pieces = 4 if n < 2 else 1
        size = refs[n].shape[0] // pieces
        for piece in range(pieces):
            rows = pl.ds(piece * size, size)
            copies.append(
                pltpu.make_async_copy(
                    refs[n].at[rows], refs[count + n].at[rows], sems.at[len(copies)]
                )
            )
    for copy in copies:
        copy.start()
    for copy in copies:
        copy.wait()


def solution(mesh):
    nx, ny = mesh.shape["gx"], mesh.shape["gy"]
    vmem = pl.BlockSpec(memory_space=pltpu.VMEM)
    anywhere = pl.BlockSpec(memory_space=pl.ANY)
    dma = pltpu.SemaphoreType.DMA

    def per_device(feat, cot, offsets, adjacency, near_w, link_w, top_w, top_k):
        scratch = [
            pltpu.VMEM((C, N, N), bf16),
            pltpu.VMEM((C, N, N), bf16),
            pltpu.VMEM((B, L, N), jnp.int32),
            pltpu.VMEM((2, K), jnp.int32),
            pltpu.VMEM((K, C, C), bf16),
            pltpu.VMEM((L, C, C), bf16),
            pltpu.VMEM((C, C), bf16),
            pltpu.VMEM((N, N), f32),
            pltpu.VMEM((W, HALO, C, N), bf16),
            pltpu.VMEM((W, HALO, C, N), bf16),
            pltpu.VMEM((2, 2, C, N), bf16),
            pltpu.VMEM((2, 2, C, N), bf16),
            pltpu.VMEM((4, C, N), bf16),
            pltpu.VMEM((4, C, N), bf16),
            pltpu.VMEM((4, C, N), bf16),
            pltpu.VMEM((4, C, N), bf16),
            pltpu.VMEM((K, C, N), f32),
            pltpu.VMEM((K, C, N), f32),
            pltpu.VMEM((W * W, C, N), bf16),
            pltpu.VMEM((W * W, C, N), bf16),
            pltpu.VMEM((GROUP * C, W * BAND * C), bf16),
            pltpu.VMEM((GROUP * C, W * BAND * C), bf16),
            pltpu.VMEM((N, B * N), bf16),
            pltpu.VMEM((C, B * N), f32),
            pltpu.VMEM((L, TARGETS, N), bf16),
            pltpu.VMEM((L, N), jnp.int32),
            pltpu.VMEM((9, C, N), bf16),
            pltpu.VMEM((L, C, N), bf16),
            pltpu.VMEM((B, C, N), f32),
            pltpu.VMEM((ny, 8, N), f32),
            pltpu.VMEM((nx, ny, N), f32),
            pltpu.VMEM((ny, 8, N), f32),
            pltpu.VMEM((nx, ny, N), f32),
            pltpu.VMEM((5, C, N), f32),
            pltpu.VMEM((9, C, N), f32),
            pltpu.VMEM((W, BAND * C, GROUP * C), f32),
            pltpu.VMEM((ny, 48, N), bf16),
            pltpu.VMEM((ny, 48, N), bf16),
            pltpu.VMEM((nx, 48, N), bf16),
            pltpu.VMEM((ny, 48, N), bf16),
            pltpu.VMEM((C, N), f32),
            pltpu.VMEM((K, N), jnp.int32),
            pltpu.VMEM((2 * N, 4 * N), bf16),
            pltpu.VMEM((8, C, N), bf16),
            pltpu.VMEM((N // (2 * GROUP), GROUP * C, 2 * N), f32),
            pltpu.VMEM((W * W, 32, N), f32),
            dma((11,)),
            dma((8,)), dma((8,)), dma((8,)), dma((8,)),
            dma((8,)), dma((8,)), dma((8,)), dma((8,)),
            dma((ny,)), dma((ny,)), dma((nx,)), dma((nx,)),
            dma((ny,)), dma((ny,)), dma((nx,)), dma((nx,)),
            dma((ny,)), dma((ny,)), dma((nx,)), dma((nx,)), dma((ny,)), dma((ny,)),
        ]
        results = (
            ((C, N, N), bf16),
            ((C, N, N), bf16),
            ((K, C, C), f32),
            ((L, C, C), f32),
            ((C, C), f32),
        )
        held = pl.pallas_call(
            functools.partial(kernel, nx, ny),
            out_shape=[pltpu.VMEM(*result) for result in results],
            in_specs=[
                anywhere, anywhere, anywhere, anywhere,
                pl.BlockSpec(memory_space=pltpu.SMEM),
                anywhere, anywhere, anywhere, anywhere,
            ],
            out_specs=[vmem] * 5,
            scratch_shapes=scratch,
            compiler_params=pltpu.CompilerParams(
                collective_id=0, has_side_effects=True, vmem_limit_bytes=54 * 2**20
            ),
        )(
            feat, cot, jnp.transpose(adjacency, (0, 2, 1)), offsets.T, offsets.T, near_w, link_w,
            top_w, top_k,
        )
        return pl.pallas_call(
            store,
            out_shape=[jax.ShapeDtypeStruct(*result) for result in results],
            in_specs=[vmem] * 5,
            out_specs=[anywhere] * 5,
            scratch_shapes=[dma((11,))],
            compiler_params=pltpu.CompilerParams(vmem_limit_bytes=2**20),
        )(*[pltpu.with_memory_space_constraint(value, pltpu.VMEM) for value in held])

    return jax.shard_map(
        per_device,
        mesh=mesh,
        in_specs=(P(None, "gx", "gy"), P(None, "gx", "gy"), P(), P(), P(), P(), P(), P()),
        out_specs=(P(None, "gx", "gy"), P(None, "gx", "gy"), P(), P(), P()),
        check_vma=False,
    )
```

```python
import functools

import jax
import jax.numpy as jnp
from jax import lax
from jax.experimental import pallas as pl
from jax.experimental.pallas import tpu as pltpu
from jax.sharding import PartitionSpec as P

C = 64
N = 128
K = 16
L = 8
CELL = 16
B = 8
W = 5
R = 2
HALO = N + 2 * R
GROUP = 4
BAND = GROUP + 2 * R
SLABS = 66
TARGETS = 640

root_scale = 0.7978845608028654
cubic_term = 0.044715

bf16 = jnp.bfloat16
f32 = jnp.float32
MESH = pl.DeviceIdType.MESH
HIGHEST = lax.Precision.HIGHEST
NT = (((1,), (1,)), ((), ()))
NN = (((1,), (0,)), ((), ()))
TN = (((0,), (0,)), ((), ()))


def dot(a, b, dims=NN, precision=None):
    return lax.dot_general(a, b, dims, preferred_element_type=f32, precision=precision)


def split_dot(a, b, dims=NN, terms=3):
    total = None
    for _ in range(terms):
        high = a.astype(bf16)
        part = dot(high, b, dims)
        total = part if total is None else total + part
        a = a - high.astype(f32)
    return total


def dot_split(a, b, dims=NN, terms=2):
    total = None
    for _ in range(terms):
        high = b.astype(bf16)
        part = dot(a, high, dims)
        total = part if total is None else total + part
        b = b - high.astype(f32)
    return total


def kernel(
    nx, ny,
    feat, cot, adj, offs_in, spots, nw_in, lw_in, tw_in, tk_in,
    obuf, ibuf, near_out, link_out, top_out,
    fbuf, cbuf, abuf, offs, nw, lw, tw, tk, xs, hs, xpack, hpack, xright, xleft, hright, hleft,
    wide, wide_t, w5, w5t, fwd, bwd, spread, pooled, onehot, idx,
    coarse_nb, picked, base, top1, top2, two1, two2, ctr, rctr, grads,
    rs_src, rs1, rs2, ag, one_ref, codes, mover, edges, near_buf, stencil,
    load_sem, halo_s, halo_r, hhalo_s, hhalo_r, co_s, co_r, ct_s, ct_r,
    t1_s, t1_r, t2_s, t2_r, u1_s, u1_r, u2_s, u2_r,
    r1_s, r1_r, r2_s, r2_r, a1_s, a1_r,
):
    gx = lax.axis_index("gx")
    gy = lax.axis_index("gy")

    def at(dx, dy):
        return (lax.rem(gx + dx + nx, nx), lax.rem(gy + dy + ny, ny))

    quarter = N // 4
    field_loads = [
        pltpu.make_async_copy(
            feat.at[:, pl.ds(n * quarter, quarter), :], fbuf.at[:, pl.ds(n * quarter, quarter), :],
            load_sem.at[n],
        )
        for n in range(4)
    ]
    loads = field_loads + [
        pltpu.make_async_copy(source, target, load_sem.at[4 + n])
        for n, (source, target) in enumerate(
            (
                (offs_in, offs), (nw_in, nw), (adj.at[pl.ds(gx * B, B)], abuf), (lw_in, lw),
                (tw_in, tw), (tk_in, tk), (cot, cbuf),
            )
        )
    ]
    for load in loads:
        load.start()

    barrier = pltpu.get_barrier_semaphore()
    for j in range(1, nx):
        pl.semaphore_signal(barrier, inc=1, device_id=at(j, 0), device_id_type=MESH)
    for j in range(1, ny):
        pl.semaphore_signal(barrier, inc=1, device_id=at(0, j), device_id_type=MESH)
    for dx in (-1, 1):
        for dy in (-1, 1):
            pl.semaphore_signal(barrier, inc=1, device_id=at(dx, dy), device_id_type=MESH)

    lane = lax.broadcasted_iota(jnp.int32, (C, N), 1)
    low = lane < C

    def build_spread(i, carry):
        rows = lax.broadcasted_iota(jnp.int32, (N, N), 0) % C
        cols = lax.broadcasted_iota(jnp.int32, (N, N), 1) // CELL + i * B
        hit = jnp.where(rows == cols, 1.0, 0.0).astype(bf16)
        spread[:, pl.ds(pl.multiple_of(i * N, N), N)] = hit
        return carry

    lax.fori_loop(0, B, build_spread, 0)
    xpack[...] = jnp.zeros_like(xpack)

    def pack_edges(block, i, pack):
        first = jnp.zeros((C, N), bf16)
        last = jnp.zeros((C, N), bf16)
        for x in range(CELL):
            turned = pltpu.roll(block[x], 2 * x, 1) if x else block[x]
            first = jnp.where((lane >= 2 * x) & (lane < 2 * x + 2), turned, first)
            spot = (2 * x - 2) % N
            last = jnp.where((lane >= spot) & (lane < spot + 2), turned, last)
        shift = 2 * CELL * (i % 4)
        half = i // 4
        pack[0, half] = pack[0, half] + pltpu.roll(first, shift, 1)
        pack[1, half] = pack[1, half] + pltpu.roll(last, shift + 2, 1)


    def arrange(i, carry):
        block = jnp.swapaxes(fbuf[:, pl.ds(pl.multiple_of(i * CELL, CELL), CELL), :], 0, 1)
        xs[R, pl.ds(R + i * CELL, CELL)] = block
        total = block[0].astype(f32)
        for x in range(1, CELL):
            total = total + block[x].astype(f32)
        pooled[:, pl.ds(pl.multiple_of(i * N, N), N)] = total
        pack_edges(block, i, xpack)
        return carry

    for n in range(4):
        field_loads[n].wait()
        lax.fori_loop(2 * n, 2 * n + 2, arrange, 0)

    def halo_copies(field, pack, right, left, send, recv):
        mid = field.at[R]
        plan = [
            (mid.at[pl.ds(R, R)], mid.at[pl.ds(R + N, R)], (-1, 0)),
            (mid.at[pl.ds(N, R)], mid.at[pl.ds(0, R)], (1, 0)),
            (pack.at[0], right.at[pl.ds(1, 2)], (0, -1)),
            (pack.at[1], left.at[pl.ds(1, 2)], (0, 1)),
            (pack.at[0, 0], right.at[3], (-1, -1)),
            (pack.at[0, 1], right.at[0], (1, -1)),
            (pack.at[1, 0], left.at[3], (-1, 1)),
            (pack.at[1, 1], left.at[0], (1, 1)),
        ]
        return [
            pltpu.make_async_remote_copy(
                src_ref=src, dst_ref=dst, send_sem=send.at[n], recv_sem=recv.at[n],
                device_id=at(*way), device_id_type=MESH,
            )
            for n, (src, dst, way) in enumerate(plan)
        ]

    def finish_halo(field, right, left):
        up, down = gx > 0, gx < nx - 1
        field[R, pl.ds(0, R)] = jnp.where(up, field[R, pl.ds(0, R)], jnp.zeros((R, C, N), bf16))
        field[R, pl.ds(R + N, R)] = jnp.where(
            down, field[R, pl.ds(R + N, R)], jnp.zeros((R, C, N), bf16)
        )
        for side, inside in ((right, gy < ny - 1), (left, gy > 0)):
            for part, there in ((0, inside & up), (1, inside), (2, inside), (3, inside & down)):
                side[part] = jnp.where(there, side[part], jnp.zeros((C, N), bf16))

        for part in range(4):
            for half in range(2):
                one, two = (left[part], pltpu.roll(right[part], C, 1))
                if half:
                    one, two = (pltpu.roll(left[part], C, 1), right[part])
                edges[2 * part + half] = jnp.where(low, one, two)

        def shift(step, carry):
            rows = []
            for n in range(SLABS):
                t = step * SLABS + n
                place = t + (C - R)
                turn = lax.rem(N - 2 * lax.rem(place, 32), N)
                rows.append(
                    jnp.concatenate([field[R, t], pltpu.roll(edges[place // 32], turn, 1)], axis=1)
                )
            moved = dot(jnp.concatenate(rows, axis=0), mover[...]).astype(bf16)
            for n, o in enumerate((0, 1, 3, 4)):
                field[o, pl.ds(step * SLABS, SLABS)] = moved[:, n * N : (n + 1) * N].reshape(
                    SLABS, C, N
                )
            return carry

        lax.fori_loop(0, HALO // SLABS, shift, 0)

    def around():
        return [(dx, dy) for dx in (-1, 0, 1) for dy in (-1, 0, 1) if (dx, dy) != (0, 0)]

    def line(axis, src, dst, send, recv):
        n = nx if axis == "gx" else ny
        me = gx if axis == "gx" else gy

        def copy(j, source, target):
            peer = lax.rem(me + j, n)
            return pltpu.make_async_remote_copy(
                src_ref=src(source(peer)), dst_ref=dst(target), send_sem=send.at[j],
                recv_sem=recv.at[j],
                device_id=(peer, gy) if axis == "gx" else (gx, peer), device_id_type=MESH,
            )

        def start():
            def step(j, carry):
                copy(j, lambda peer: peer, me).start()
                return carry

            lax.fori_loop(1, n, step, 0)

        def wait():
            def step(j, carry):
                copy(j, lambda peer: peer, lax.rem(me + n - j, n)).wait_recv()
                copy(j, lambda peer: peer, me).wait_send()
                return carry

            lax.fori_loop(1, n, step, 0)

        return start, wait

    pl.semaphore_wait(barrier, nx - 1 + ny - 1 + 4)
    xhalo = halo_copies(xs, xpack, xright, xleft, halo_s, halo_r)
    for copy in xhalo:
        copy.start()

    coarse = (split_dot(pooled[...], spread[...], NT) / CELL).astype(bf16)
    coarse_nb[4] = coarse
    ones = jnp.where(lax.broadcasted_iota(jnp.int32, (8, N), 1) < C, 1.0, 0.0)

    def as_row(values):
        sums = dot(ones, values, NT, HIGHEST)
        return jnp.concatenate([sums, jnp.zeros((8, N - C), f32)], axis=1)

    top1[gy] = as_row(coarse.astype(f32)) / B

    coarse_copies = []
    for n, (dx, dy) in enumerate(around()):
        slot = (1 - dx) * 3 + (1 - dy)
        copy = pltpu.make_async_remote_copy(
            src_ref=coarse_nb.at[4], dst_ref=coarse_nb.at[slot], send_sem=co_s.at[n],
            recv_sem=co_r.at[n], device_id=at(dx, dy), device_id_type=MESH,
        )
        copy.start()
        coarse_copies.append(copy)
    t1_start, t1_wait = line("gy", lambda p: top1.at[gy], lambda p: top1.at[p], t1_s, t1_r)
    t1_start()

    hpack[...] = jnp.zeros_like(hpack)
    source = lax.broadcasted_iota(jnp.int32, (2 * N, N), 0)
    for n, o in enumerate((0, 1, 3, 4)):
        y = lax.broadcasted_iota(jnp.int32, (2 * N, N), 1) + (o - R)
        y = jnp.where(y < 0, y + N + R, jnp.where(y >= N, y + C, y))
        mover[:, n * N : (n + 1) * N] = jnp.where(source == y, 1.0, 0.0).astype(bf16)
    for load in loads[4:]:
        load.wait()
    def widen(k, carry):
        block = nw[k].astype(f32)
        wide[k] = jnp.concatenate([block, block], axis=1)
        turned = block.T
        wide_t[k] = jnp.concatenate([turned, turned], axis=1)
        return carry

    lax.fori_loop(0, K, widen, 0, unroll=4)

    code = (offs[pl.ds(0, 1), :] + R) * W + offs[pl.ds(1, 1), :] + R

    def coded(points, stride, first):
        row = lax.broadcasted_iota(jnp.int32, (points, K), 0) * stride + first
        col = lax.broadcasted_iota(jnp.int32, (points, K), 1)
        hit = jnp.where(row == col, jnp.broadcast_to(code, (points, K)).astype(f32), 0.0)
        own = jnp.sum(hit, axis=1, keepdims=True).astype(jnp.int32)
        return jnp.broadcast_to(own, (points, N))

    codes[...] = coded(K, 1, 0)

    def place(p, carry):
        plain = jnp.zeros((C, N), f32)
        turned = jnp.zeros((C, N), f32)
        for k in range(K):
            mine = codes[pl.ds(k, 1), :] == p
            plain = plain + jnp.where(mine, wide[k], 0.0)
            turned = turned + jnp.where(mine, wide_t[k], 0.0)
        w5[p] = plain.astype(bf16)
        w5t[p] = turned.astype(bf16)
        return carry

    lax.fori_loop(0, W * W, place, 0, unroll=5)
    nothing = jnp.zeros((C, N), bf16)

    def band(o, carry):
        for s in range(GROUP):
            for j in range(BAND // 2):
                ahead, back = [], []
                for r in (2 * j, 2 * j + 1):
                    a = r - s
                    inside = 0 <= a < W
                    ahead.append(w5t[a * W + o] if inside else nothing)
                    back.append(w5[(W - 1 - a) * W + (W - 1 - o)] if inside else nothing)
                cols = pl.ds(pl.multiple_of(o * BAND * C + j * N, N), N)
                fwd[pl.ds(s * C, C), cols] = jnp.where(low, ahead[0], ahead[1])
                bwd[pl.ds(s * C, C), cols] = jnp.where(low, back[0], back[1])
        return carry

    lax.fori_loop(0, W, band, 0, unroll=True)

    lane8 = lax.broadcasted_iota(jnp.int32, (L, N), 1)
    found = jnp.zeros((L, N), jnp.int32)
    for i in range(B):
        turned = pltpu.roll(abuf[i], lax.rem(N + i * B - gy * B, N), 1)
        found = jnp.where((lane8 >= i * B) & (lane8 < i * B + B), turned, found)
    rows = (found >> 7) - gx * B + B
    cols = (found & 127) - gy * B + B
    spot = ((rows >> 3) * 3 + (cols >> 3)) * C + (rows & 7) * B + (cols & 7)
    idx[...] = jnp.where(lane8 < C, spot, -1)

    def build_onehot(l, carry):
        target = lax.broadcasted_iota(jnp.int32, (TARGETS, N), 0)
        onehot[l] = jnp.where(target == idx[pl.ds(l, 1), :], 1.0, 0.0).astype(bf16)
        return carry

    lax.fori_loop(0, L, build_onehot, 0)

    t1_wait()
    top2[gx] = top1[:, 0, :]
    t2_start, t2_wait = line("gx", lambda p: top2.at[gx], lambda p: top2.at[p], t2_s, t2_r)
    t2_start()

    for copy in xhalo:
        copy.wait()
    finish_halo(xs, xright, xleft)

    for copy in coarse_copies:
        copy.wait()
    pieces = [
        jnp.where(low, coarse_nb[2 * j], coarse_nb[2 * j + 1] if j < 4 else nothing)
        for j in range(5)
    ]
    around_cells = jnp.concatenate(pieces, axis=1)

    def pick(l, total):
        chosen = dot(around_cells, onehot[l]).astype(bf16)
        picked[l] = chosen
        turned = lw[l].astype(f32).T.astype(bf16)
        return total + dot(turned, chosen)

    def banded(matrix, field, pair):
        parts = []
        for o in range(W):
            first = field[o, pl.ds(pair * 8, BAND)].reshape(BAND * C, N)
            second = field[o, pl.ds(pair * 8 + GROUP, BAND)].reshape(BAND * C, N)
            parts.append(jnp.concatenate([first, second], axis=1))
        return dot(matrix[...], jnp.concatenate(parts, axis=0))

    def near_field(pair):
        near_buf[pair] = banded(fwd, xs, pair)

    for pair in range(B // 2):
        near_field(pair)
    level_one = lax.fori_loop(0, L, pick, jnp.zeros((C, N), f32), unroll=True)
    for pair in range(B // 2, B):
        near_field(pair)
    t2_wait()
    me = gx * ny + gy
    top_all = top2[...].reshape(N, N)
    tw_f32 = tw[...].astype(f32)
    mixed = dot(tw_f32.T, top_all[:, :C], NT, HIGHEST)
    level_two = jnp.sum(mixed * tk[pl.ds(me, 1), :], axis=1, keepdims=True)
    spread_one = split_dot(level_one[:, :C], spread[pl.ds(0, C), :]) + level_two
    for i in range(B):
        base[i] = spread_one[:, i * N : (i + 1) * N]


    def forward(i):
        rows16 = pl.ds(i * CELL, CELL)
        upstream = jnp.swapaxes(cbuf[:, rows16, :], 0, 1)
        shared = base[i]
        actives = []
        total = jnp.zeros((C, N), f32)
        for half in range(2):
            for g in range(2):
                for s in range(GROUP):
                    x = half * 8 + g * GROUP + s
                    near = near_buf[i * 2 + half, pl.ds(s * C, C), pl.ds(g * N, N)]
                    v = near + shared
                    square = v * v
                    tangent = jnp.tanh(v * (root_scale + root_scale * cubic_term * square))
                    gate = 0.5 + 0.5 * tangent
                    own = xs[R, R + i * CELL + x].astype(f32)
                    actives.append((own + v * gate).astype(bf16))
                    slope = gate + v * (gate - gate * gate) * (
                        2.0 * root_scale + 6.0 * root_scale * cubic_term * square
                    )
                    grad = (upstream[x].astype(f32) * slope).astype(bf16)
                    hs[R, R + i * CELL + x] = grad
                    total = total + grad.astype(f32)
        pooled[:, pl.ds(i * N, N)] = total
        obuf[:, rows16, :] = jnp.swapaxes(jnp.stack(actives), 0, 1)

    def weigh(o, half):
        groups = [half * (N // GROUP // 2) + i for i in range(N // GROUP // 2)]
        left = jnp.concatenate(
            [xs[o, pl.ds(i * GROUP, BAND)].reshape(BAND * C, N) for i in groups], axis=1
        )
        right = jnp.concatenate(
            [hs[R, pl.ds(R + i * GROUP, GROUP)].reshape(GROUP * C, N) for i in groups], axis=1
        )
        return dot(left, right, NT)

    for i in range(B // 2):
        near_field(B + 2 * i)
        near_field(B + 2 * i + 1)
        forward(i)
    for i in range(B // 2):
        grads[i] = weigh(i, 0)
        forward(B // 2 + i)

    one = split_dot(pooled[...], spread[...], NT)
    one_ref[...] = one
    for o in range(W):
        grads[o] = weigh(o, 1) + (grads[o] if o < B // 2 else weigh(o, 0))
    def stencil_grad(p, carry):
        a = p // W
        b = lax.rem(p, W)
        part = [
            grads[b, pl.ds(pl.multiple_of((a + s) * C, C), C), pl.ds((s // 2) * N, N)]
            for s in range(GROUP)
        ]
        both = jnp.where(low, part[0] + part[2], part[1] + part[3])
        both = both + pltpu.roll(both, C, 1)
        stencil[p] = jnp.where(low[:32], both[:32], both[32:])
        return carry

    lax.fori_loop(0, W * W, stencil_grad, 0, unroll=True)

    for k in range(K):
        rs_src[k, pl.ds(0, 32), :] = stencil[(spots[0, k] + R) * W + spots[1, k] + R].astype(bf16)

    def link_grads(l, carry):
        grad = dot_split(picked[l], one_ref[...], NT)
        for half in range(2):
            rows = [grad[(2 * half + n) * 16 : (2 * half + n + 1) * 16] for n in range(2)]
            rs_src[2 * l + half, pl.ds(32, 16), :] = jnp.concatenate(
                [rows[0][:, :C], rows[1][:, :C]], axis=1
            ).astype(bf16)
        return carry

    lax.fori_loop(0, L, link_grads, 0, unroll=True)
    rs1[gy] = rs_src[gy]
    r1_start, r1_wait = line("gy", lambda p: rs_src.at[p], lambda p: rs1.at[p], r1_s, r1_r)
    r1_start()
    two1[gy] = as_row(one_ref[...])
    u1_start, u1_wait = line("gy", lambda p: two1.at[gy], lambda p: two1.at[p], u1_s, u1_r)
    u1_start()

    def pack_hidden(i, carry):
        pack_edges(hs[R, pl.ds(R + i * CELL, CELL)], i, hpack)
        return carry

    lax.fori_loop(0, B, pack_hidden, 0)
    hhalo = halo_copies(hs, hpack, hright, hleft, hhalo_s, hhalo_r)
    for copy in hhalo:
        copy.start()

    def push(l, total):
        grad = one_ref[...]
        pushed = dot_split(lw[l], grad)
        return total + split_dot(pushed, onehot[l], NT, 2)

    pushes = lax.fori_loop(0, L, push, jnp.zeros((C, TARGETS), f32), unroll=True)
    for j in range(5):
        ctr[j] = pushes[:, j * N : (j + 1) * N]
    push_copies = []
    for n, (dx, dy) in enumerate(around()):
        slot = (1 - dx) * 3 + (1 - dy)
        copy = pltpu.make_async_remote_copy(
            src_ref=ctr.at[(8 - slot) // 2], dst_ref=rctr.at[slot], send_sem=ct_s.at[n],
            recv_sem=ct_r.at[n], device_id=at(dx, dy), device_id_type=MESH,
        )
        copy.start()
        push_copies.append(copy)

    r1_wait()
    total = rs1[0].astype(f32)
    for j in range(1, ny):
        total = total + rs1[j].astype(f32)
    rs2[gx] = total.astype(bf16)
    r2_start, r2_wait = line("gx", lambda p: rs2.at[gx], lambda p: rs2.at[p], r2_s, r2_r)
    r2_start()
    u1_wait()
    two2[gx] = two1[:, 0, :]
    u2_start, u2_wait = line("gx", lambda p: two2.at[gx], lambda p: two2.at[p], u2_s, u2_r)
    u2_start()

    for copy in hhalo:
        copy.wait()
    finish_halo(hs, hright, hleft)

    for copy in push_copies:
        copy.wait()
    evens = ctr[2]
    odds = jnp.zeros((C, N), f32)
    for slot in range(9):
        if slot == 4:
            continue
        if slot % 2 == 0:
            evens = evens + rctr[slot]
        else:
            odds = odds + rctr[slot]
    collected = evens + pltpu.roll(odds, C, 1)
    r2_wait()
    total = rs2[0].astype(f32)
    for j in range(1, nx):
        total = total + rs2[j].astype(f32)
    ag[gy] = total.astype(bf16)
    a1_start, a1_wait = line("gy", lambda p: ag.at[gy], lambda p: ag.at[p], a1_s, a1_r)
    a1_start()
    u2_wait()
    two_all = two2[...].reshape(N, N)[:, :C]
    kernel_grad = dot(tk[...], two_all, TN, HIGHEST)
    top_all = top2[...].reshape(N, N)
    top_out[...] = dot(top_all[:, :C], kernel_grad, TN, HIGHEST)
    mine = lax.broadcasted_iota(jnp.int32, (N, C), 0) == me
    kernel_row = jnp.sum(jnp.where(mine, kernel_grad, 0.0), axis=0, keepdims=True)
    top_coef_grad = jnp.sum(tw[...].astype(f32) * kernel_row, axis=1, keepdims=True)
    coarse_grad = (collected + top_coef_grad / B) / CELL
    spread_grad = split_dot(coarse_grad[:, :C], spread[pl.ds(0, C), :])
    for i in range(B):
        base[i] = spread_grad[:, i * N : (i + 1) * N]

    def backward(i, carry):
        rows16 = pl.ds(pl.multiple_of(i * CELL, CELL), CELL)
        shared = base[i]
        sums = []
        for half in range(2):
            near = banded(bwd, hs, i * 2 + half)
            for g in range(2):
                for s in range(GROUP):
                    sums.append(near[s * C : (s + 1) * C, g * N : (g + 1) * N] + shared)
        total = jnp.swapaxes(jnp.stack(sums), 0, 1)
        ibuf[:, rows16, :] = (cbuf[:, rows16, :].astype(f32) + total).astype(bf16)
        return carry

    lax.fori_loop(0, B, backward, 0, unroll=True)
    a1_wait()
    for k in range(K):
        whole = ag[k].astype(f32)
        near_out[k, pl.ds(0, 32), :] = whole[:32, :C]
        near_out[k, pl.ds(32, 32), :] = pltpu.roll(whole[:32], C, 1)[:, :C]
        link_out[k // 2, pl.ds((k % 2) * 32, 16), :] = whole[32:, :C]
        link_out[k // 2, pl.ds((k % 2) * 32 + 16, 16), :] = pltpu.roll(whole[32:], C, 1)[:, :C]


def store(*refs):
    count = len(refs) // 2
    sems = refs[-1]
    copies = []
    for n in range(count):
        pieces = 4 if n < 2 else 1
        size = refs[n].shape[0] // pieces
        for piece in range(pieces):
            rows = pl.ds(piece * size, size)
            copies.append(
                pltpu.make_async_copy(
                    refs[n].at[rows], refs[count + n].at[rows], sems.at[len(copies)]
                )
            )
    for copy in copies:
        copy.start()
    for copy in copies:
        copy.wait()


def solution(mesh):
    nx, ny = mesh.shape["gx"], mesh.shape["gy"]
    vmem = pl.BlockSpec(memory_space=pltpu.VMEM)
    anywhere = pl.BlockSpec(memory_space=pl.ANY)
    dma = pltpu.SemaphoreType.DMA

    def per_device(feat, cot, offsets, adjacency, near_w, link_w, top_w, top_k):
        scratch = [
            pltpu.VMEM((C, N, N), bf16),
            pltpu.VMEM((C, N, N), bf16),
            pltpu.VMEM((B, L, N), jnp.int32),
            pltpu.VMEM((2, K), jnp.int32),
            pltpu.VMEM((K, C, C), bf16),
            pltpu.VMEM((L, C, C), bf16),
            pltpu.VMEM((C, C), bf16),
            pltpu.VMEM((N, N), f32),
            pltpu.VMEM((W, HALO, C, N), bf16),
            pltpu.VMEM((W, HALO, C, N), bf16),
            pltpu.VMEM((2, 2, C, N), bf16),
            pltpu.VMEM((2, 2, C, N), bf16),
            pltpu.VMEM((4, C, N), bf16),
            pltpu.VMEM((4, C, N), bf16),
            pltpu.VMEM((4, C, N), bf16),
            pltpu.VMEM((4, C, N), bf16),
            pltpu.VMEM((K, C, N), f32),
            pltpu.VMEM((K, C, N), f32),
            pltpu.VMEM((W * W, C, N), bf16),
            pltpu.VMEM((W * W, C, N), bf16),
            pltpu.VMEM((GROUP * C, W * BAND * C), bf16),
            pltpu.VMEM((GROUP * C, W * BAND * C), bf16),
            pltpu.VMEM((N, B * N), bf16),
            pltpu.VMEM((C, B * N), f32),
            pltpu.VMEM((L, TARGETS, N), bf16),
            pltpu.VMEM((L, N), jnp.int32),
            pltpu.VMEM((9, C, N), bf16),
            pltpu.VMEM((L, C, N), bf16),
            pltpu.VMEM((B, C, N), f32),
            pltpu.VMEM((ny, 8, N), f32),
            pltpu.VMEM((nx, ny, N), f32),
            pltpu.VMEM((ny, 8, N), f32),
            pltpu.VMEM((nx, ny, N), f32),
            pltpu.VMEM((5, C, N), f32),
            pltpu.VMEM((9, C, N), f32),
            pltpu.VMEM((W, BAND * C, GROUP * C), f32),
            pltpu.VMEM((ny, 48, N), bf16),
            pltpu.VMEM((ny, 48, N), bf16),
            pltpu.VMEM((nx, 48, N), bf16),
            pltpu.VMEM((ny, 48, N), bf16),
            pltpu.VMEM((C, N), f32),
            pltpu.VMEM((K, N), jnp.int32),
            pltpu.VMEM((2 * N, 4 * N), bf16),
            pltpu.VMEM((8, C, N), bf16),
            pltpu.VMEM((N // (2 * GROUP), GROUP * C, 2 * N), f32),
            pltpu.VMEM((W * W, 32, N), f32),
            dma((11,)),
            dma((8,)), dma((8,)), dma((8,)), dma((8,)),
            dma((8,)), dma((8,)), dma((8,)), dma((8,)),
            dma((ny,)), dma((ny,)), dma((nx,)), dma((nx,)),
            dma((ny,)), dma((ny,)), dma((nx,)), dma((nx,)),
            dma((ny,)), dma((ny,)), dma((nx,)), dma((nx,)), dma((ny,)), dma((ny,)),
        ]
        results = (
            ((C, N, N), bf16),
            ((C, N, N), bf16),
            ((K, C, C), f32),
            ((L, C, C), f32),
            ((C, C), f32),
        )
        held = pl.pallas_call(
            functools.partial(kernel, nx, ny),
            out_shape=[pltpu.VMEM(*result) for result in results],
            in_specs=[
                anywhere, anywhere, anywhere, anywhere,
                pl.BlockSpec(memory_space=pltpu.SMEM),
                anywhere, anywhere, anywhere, anywhere,
            ],
            out_specs=[vmem] * 5,
            scratch_shapes=scratch,
            compiler_params=pltpu.CompilerParams(
                collective_id=0, has_side_effects=True, vmem_limit_bytes=54 * 2**20
            ),
        )(
            feat, cot, jnp.transpose(adjacency, (0, 2, 1)), offsets.T, offsets.T, near_w, link_w,
            top_w, top_k,
        )
        return pl.pallas_call(
            store,
            out_shape=[jax.ShapeDtypeStruct(*result) for result in results],
            in_specs=[vmem] * 5,
            out_specs=[anywhere] * 5,
            scratch_shapes=[dma((11,))],
            compiler_params=pltpu.CompilerParams(vmem_limit_bytes=2**20),
        )(*[pltpu.with_memory_space_constraint(value, pltpu.VMEM) for value in held])

    return jax.shard_map(
        per_device,
        mesh=mesh,
        in_specs=(P(None, "gx", "gy"), P(None, "gx", "gy"), P(), P(), P(), P(), P(), P()),
        out_specs=(P(None, "gx", "gy"), P(None, "gx", "gy"), P(), P(), P()),
        check_vma=False,
    )
```

```python
import functools

import jax
import jax.numpy as jnp
from jax import lax
from jax.experimental import pallas as pl
from jax.experimental.pallas import tpu as pltpu
from jax.sharding import PartitionSpec as P

C = 64
N = 128
K = 16
L = 8
CELL = 16
B = 8
W = 5
R = 2
HALO = N + 2 * R
GROUP = 4
BAND = GROUP + 2 * R
SLABS = 66
TARGETS = 640

root_scale = 0.7978845608028654
cubic_term = 0.044715

bf16 = jnp.bfloat16
f32 = jnp.float32
MESH = pl.DeviceIdType.MESH
HIGHEST = lax.Precision.HIGHEST
NT = (((1,), (1,)), ((), ()))
NN = (((1,), (0,)), ((), ()))
TN = (((0,), (0,)), ((), ()))


def dot(a, b, dims=NN, precision=None):
    return lax.dot_general(a, b, dims, preferred_element_type=f32, precision=precision)


def split_dot(a, b, dims=NN, terms=3):
    total = None
    for _ in range(terms):
        high = a.astype(bf16)
        part = dot(high, b, dims)
        total = part if total is None else total + part
        a = a - high.astype(f32)
    return total


def dot_split(a, b, dims=NN, terms=2):
    total = None
    for _ in range(terms):
        high = b.astype(bf16)
        part = dot(a, high, dims)
        total = part if total is None else total + part
        b = b - high.astype(f32)
    return total


def kernel(
    nx, ny,
    feat, cot, adj, offs_in, spots, nw_in, lw_in, tw_in, tk_in,
    obuf, ibuf, near_out, link_out, top_out,
    fbuf, cbuf, abuf, offs, nw, lw, tw, tk, xs, hs, xpack, hpack, xright, xleft, hright, hleft,
    wide, wide_t, w5, w5t, fwd, bwd, spread, pooled, onehot, idx,
    coarse_nb, picked, base, top1, top2, two1, two2, ctr, rctr, grads,
    rs_src, rs1, rs2, ag, one_ref, codes, mover, edges, near_buf, stencil,
    load_sem, halo_s, halo_r, hhalo_s, hhalo_r, co_s, co_r, ct_s, ct_r,
    t1_s, t1_r, t2_s, t2_r, u1_s, u1_r, u2_s, u2_r,
    r1_s, r1_r, r2_s, r2_r, a1_s, a1_r,
):
    gx = lax.axis_index("gx")
    gy = lax.axis_index("gy")

    def at(dx, dy):
        return (lax.rem(gx + dx + nx, nx), lax.rem(gy + dy + ny, ny))

    quarter = N // 4
    field_loads = [
        pltpu.make_async_copy(
            feat.at[:, pl.ds(n * quarter, quarter), :], fbuf.at[:, pl.ds(n * quarter, quarter), :],
            load_sem.at[n],
        )
        for n in range(4)
    ]
    loads = field_loads + [
        pltpu.make_async_copy(source, target, load_sem.at[4 + n])
        for n, (source, target) in enumerate(
            (
                (offs_in, offs), (nw_in, nw), (adj.at[pl.ds(gx * B, B)], abuf), (lw_in, lw),
                (tw_in, tw), (tk_in, tk), (cot, cbuf),
            )
        )
    ]
    for load in loads:
        load.start()

    barrier = pltpu.get_barrier_semaphore()
    for j in range(1, nx):
        pl.semaphore_signal(barrier, inc=1, device_id=at(j, 0), device_id_type=MESH)
    for j in range(1, ny):
        pl.semaphore_signal(barrier, inc=1, device_id=at(0, j), device_id_type=MESH)
    for dx in (-1, 1):
        for dy in (-1, 1):
            pl.semaphore_signal(barrier, inc=1, device_id=at(dx, dy), device_id_type=MESH)

    lane = lax.broadcasted_iota(jnp.int32, (C, N), 1)
    low = lane < C

    def build_spread(i, carry):
        rows = lax.broadcasted_iota(jnp.int32, (N, N), 0) % C
        cols = lax.broadcasted_iota(jnp.int32, (N, N), 1) // CELL + i * B
        hit = jnp.where(rows == cols, 1.0, 0.0).astype(bf16)
        spread[:, pl.ds(pl.multiple_of(i * N, N), N)] = hit
        return carry

    lax.fori_loop(0, B, build_spread, 0)
    xpack[...] = jnp.zeros_like(xpack)

    def pack_edges(block, i, pack):
        first = jnp.zeros((C, N), bf16)
        last = jnp.zeros((C, N), bf16)
        for x in range(CELL):
            turned = pltpu.roll(block[x], 2 * x, 1) if x else block[x]
            first = jnp.where((lane >= 2 * x) & (lane < 2 * x + 2), turned, first)
            spot = (2 * x - 2) % N
            last = jnp.where((lane >= spot) & (lane < spot + 2), turned, last)
        shift = 2 * CELL * (i % 4)
        half = i // 4
        pack[0, half] = pack[0, half] + pltpu.roll(first, shift, 1)
        pack[1, half] = pack[1, half] + pltpu.roll(last, shift + 2, 1)


    def arrange(i, carry):
        block = jnp.swapaxes(fbuf[:, pl.ds(pl.multiple_of(i * CELL, CELL), CELL), :], 0, 1)
        xs[R, pl.ds(R + i * CELL, CELL)] = block
        total = block[0].astype(f32)
        for x in range(1, CELL):
            total = total + block[x].astype(f32)
        pooled[:, pl.ds(pl.multiple_of(i * N, N), N)] = total
        pack_edges(block, i, xpack)
        return carry

    for n in range(4):
        field_loads[n].wait()
        lax.fori_loop(2 * n, 2 * n + 2, arrange, 0)

    def halo_copies(field, pack, right, left, send, recv):
        mid = field.at[R]
        plan = [
            (mid.at[pl.ds(R, R)], mid.at[pl.ds(R + N, R)], (-1, 0)),
            (mid.at[pl.ds(N, R)], mid.at[pl.ds(0, R)], (1, 0)),
            (pack.at[0], right.at[pl.ds(1, 2)], (0, -1)),
            (pack.at[1], left.at[pl.ds(1, 2)], (0, 1)),
            (pack.at[0, 0], right.at[3], (-1, -1)),
            (pack.at[0, 1], right.at[0], (1, -1)),
            (pack.at[1, 0], left.at[3], (-1, 1)),
            (pack.at[1, 1], left.at[0], (1, 1)),
        ]
        return [
            pltpu.make_async_remote_copy(
                src_ref=src, dst_ref=dst, send_sem=send.at[n], recv_sem=recv.at[n],
                device_id=at(*way), device_id_type=MESH,
            )
            for n, (src, dst, way) in enumerate(plan)
        ]

    def finish_halo(field, right, left):
        up, down = gx > 0, gx < nx - 1
        field[R, pl.ds(0, R)] = jnp.where(up, field[R, pl.ds(0, R)], jnp.zeros((R, C, N), bf16))
        field[R, pl.ds(R + N, R)] = jnp.where(
            down, field[R, pl.ds(R + N, R)], jnp.zeros((R, C, N), bf16)
        )
        for side, inside in ((right, gy < ny - 1), (left, gy > 0)):
            for part, there in ((0, inside & up), (1, inside), (2, inside), (3, inside & down)):
                side[part] = jnp.where(there, side[part], jnp.zeros((C, N), bf16))

        for part in range(4):
            for half in range(2):
                one, two = (left[part], pltpu.roll(right[part], C, 1))
                if half:
                    one, two = (pltpu.roll(left[part], C, 1), right[part])
                edges[2 * part + half] = jnp.where(low, one, two)

        def shift(step, carry):
            rows = []
            for n in range(SLABS):
                t = step * SLABS + n
                place = t + (C - R)
                turn = lax.rem(N - 2 * lax.rem(place, 32), N)
                rows.append(
                    jnp.concatenate([field[R, t], pltpu.roll(edges[place // 32], turn, 1)], axis=1)
                )
            moved = dot(jnp.concatenate(rows, axis=0), mover[...]).astype(bf16)
            for n, o in enumerate((0, 1, 3, 4)):
                field[o, pl.ds(step * SLABS, SLABS)] = moved[:, n * N : (n + 1) * N].reshape(
                    SLABS, C, N
                )
            return carry

        lax.fori_loop(0, HALO // SLABS, shift, 0)

    def around():
        return [(dx, dy) for dx in (-1, 0, 1) for dy in (-1, 0, 1) if (dx, dy) != (0, 0)]

    def line(axis, src, dst, send, recv):
        n = nx if axis == "gx" else ny
        me = gx if axis == "gx" else gy

        def copy(j, source, target):
            peer = lax.rem(me + j, n)
            return pltpu.make_async_remote_copy(
                src_ref=src(source(peer)), dst_ref=dst(target), send_sem=send.at[j],
                recv_sem=recv.at[j],
                device_id=(peer, gy) if axis == "gx" else (gx, peer), device_id_type=MESH,
            )

        def start():
            def step(j, carry):
                copy(j, lambda peer: peer, me).start()
                return carry

            lax.fori_loop(1, n, step, 0)

        def wait():
            def step(j, carry):
                copy(j, lambda peer: peer, lax.rem(me + n - j, n)).wait_recv()
                copy(j, lambda peer: peer, me).wait_send()
                return carry

            lax.fori_loop(1, n, step, 0)

        return start, wait

    pl.semaphore_wait(barrier, nx - 1 + ny - 1 + 4)
    xhalo = halo_copies(xs, xpack, xright, xleft, halo_s, halo_r)
    for copy in xhalo:
        copy.start()

    coarse = (split_dot(pooled[...], spread[...], NT) / CELL).astype(bf16)
    coarse_nb[4] = coarse
    ones = jnp.where(lax.broadcasted_iota(jnp.int32, (8, N), 1) < C, 1.0, 0.0)

    def as_row(values):
        sums = dot(ones, values, NT, HIGHEST)
        return jnp.concatenate([sums, jnp.zeros((8, N - C), f32)], axis=1)

    top1[gy] = as_row(coarse.astype(f32)) / B

    coarse_copies = []
    for n, (dx, dy) in enumerate(around()):
        slot = (1 - dx) * 3 + (1 - dy)
        copy = pltpu.make_async_remote_copy(
            src_ref=coarse_nb.at[4], dst_ref=coarse_nb.at[slot], send_sem=co_s.at[n],
            recv_sem=co_r.at[n], device_id=at(dx, dy), device_id_type=MESH,
        )
        copy.start()
        coarse_copies.append(copy)
    t1_start, t1_wait = line("gy", lambda p: top1.at[gy], lambda p: top1.at[p], t1_s, t1_r)
    t1_start()

    hpack[...] = jnp.zeros_like(hpack)
    source = lax.broadcasted_iota(jnp.int32, (2 * N, N), 0)
    for n, o in enumerate((0, 1, 3, 4)):
        y = lax.broadcasted_iota(jnp.int32, (2 * N, N), 1) + (o - R)
        y = jnp.where(y < 0, y + N + R, jnp.where(y >= N, y + C, y))
        mover[:, n * N : (n + 1) * N] = jnp.where(source == y, 1.0, 0.0).astype(bf16)
    for load in loads[4:]:
        load.wait()
    def widen(k, carry):
        block = nw[k].astype(f32)
        wide[k] = jnp.concatenate([block, block], axis=1)
        turned = block.T
        wide_t[k] = jnp.concatenate([turned, turned], axis=1)
        return carry

    lax.fori_loop(0, K, widen, 0, unroll=4)

    code = (offs[pl.ds(0, 1), :] + R) * W + offs[pl.ds(1, 1), :] + R

    def coded(points, stride, first):
        row = lax.broadcasted_iota(jnp.int32, (points, K), 0) * stride + first
        col = lax.broadcasted_iota(jnp.int32, (points, K), 1)
        hit = jnp.where(row == col, jnp.broadcast_to(code, (points, K)).astype(f32), 0.0)
        own = jnp.sum(hit, axis=1, keepdims=True).astype(jnp.int32)
        return jnp.broadcast_to(own, (points, N))

    codes[...] = coded(K, 1, 0)

    def place(p, carry):
        plain = jnp.zeros((C, N), f32)
        turned = jnp.zeros((C, N), f32)
        for k in range(K):
            mine = codes[pl.ds(k, 1), :] == p
            plain = plain + jnp.where(mine, wide[k], 0.0)
            turned = turned + jnp.where(mine, wide_t[k], 0.0)
        w5[p] = plain.astype(bf16)
        w5t[p] = turned.astype(bf16)
        return carry

    lax.fori_loop(0, W * W, place, 0, unroll=5)
    nothing = jnp.zeros((C, N), bf16)

    def band(o, carry):
        for s in range(GROUP):
            for j in range(BAND // 2):
                ahead, back = [], []
                for r in (2 * j, 2 * j + 1):
                    a = r - s
                    inside = 0 <= a < W
                    ahead.append(w5t[a * W + o] if inside else nothing)
                    back.append(w5[(W - 1 - a) * W + (W - 1 - o)] if inside else nothing)
                cols = pl.ds(pl.multiple_of(o * BAND * C + j * N, N), N)
                fwd[pl.ds(s * C, C), cols] = jnp.where(low, ahead[0], ahead[1])
                bwd[pl.ds(s * C, C), cols] = jnp.where(low, back[0], back[1])
        return carry

    lax.fori_loop(0, W, band, 0, unroll=True)

    lane8 = lax.broadcasted_iota(jnp.int32, (L, N), 1)
    found = jnp.zeros((L, N), jnp.int32)
    for i in range(B):
        turned = pltpu.roll(abuf[i], lax.rem(N + i * B - gy * B, N), 1)
        found = jnp.where((lane8 >= i * B) & (lane8 < i * B + B), turned, found)
    rows = (found >> 7) - gx * B + B
    cols = (found & 127) - gy * B + B
    spot = ((rows >> 3) * 3 + (cols >> 3)) * C + (rows & 7) * B + (cols & 7)
    idx[...] = jnp.where(lane8 < C, spot, -1)

    def build_onehot(l, carry):
        target = lax.broadcasted_iota(jnp.int32, (TARGETS, N), 0)
        onehot[l] = jnp.where(target == idx[pl.ds(l, 1), :], 1.0, 0.0).astype(bf16)
        return carry

    lax.fori_loop(0, L, build_onehot, 0)

    t1_wait()
    top2[gx] = top1[:, 0, :]
    t2_start, t2_wait = line("gx", lambda p: top2.at[gx], lambda p: top2.at[p], t2_s, t2_r)
    t2_start()

    for copy in xhalo:
        copy.wait()
    finish_halo(xs, xright, xleft)

    for copy in coarse_copies:
        copy.wait()
    pieces = [
        jnp.where(low, coarse_nb[2 * j], coarse_nb[2 * j + 1] if j < 4 else nothing)
        for j in range(5)
    ]
    around_cells = jnp.concatenate(pieces, axis=1)

    def pick(l, total):
        chosen = dot(around_cells, onehot[l]).astype(bf16)
        picked[l] = chosen
        turned = lw[l].astype(f32).T.astype(bf16)
        return total + dot(turned, chosen)

    def banded(matrix, field, pair):
        parts = []
        for o in range(W):
            first = field[o, pl.ds(pair * 8, BAND)].reshape(BAND * C, N)
            second = field[o, pl.ds(pair * 8 + GROUP, BAND)].reshape(BAND * C, N)
            parts.append(jnp.concatenate([first, second], axis=1))
        return dot(matrix[...], jnp.concatenate(parts, axis=0))

    def near_field(pair):
        near_buf[pair] = banded(fwd, xs, pair)

    for pair in range(B // 2):
        near_field(pair)
    level_one = lax.fori_loop(0, L, pick, jnp.zeros((C, N), f32), unroll=True)
    for pair in range(B // 2, B):
        near_field(pair)
    t2_wait()
    me = gx * ny + gy
    top_all = top2[...].reshape(N, N)
    tw_f32 = tw[...].astype(f32)
    mixed = dot(tw_f32.T, top_all[:, :C], NT, HIGHEST)
    level_two = jnp.sum(mixed * tk[pl.ds(me, 1), :], axis=1, keepdims=True)
    spread_one = split_dot(level_one[:, :C], spread[pl.ds(0, C), :]) + level_two
    for i in range(B):
        base[i] = spread_one[:, i * N : (i + 1) * N]


    def forward(i):
        rows16 = pl.ds(i * CELL, CELL)
        upstream = jnp.swapaxes(cbuf[:, rows16, :], 0, 1)
        shared = base[i]
        actives = []
        total = jnp.zeros((C, N), f32)
        for half in range(2):
            for g in range(2):
                for s in range(GROUP):
                    x = half * 8 + g * GROUP + s
                    near = near_buf[i * 2 + half, pl.ds(s * C, C), pl.ds(g * N, N)]
                    v = near + shared
                    square = v * v
                    tangent = jnp.tanh(v * (root_scale + root_scale * cubic_term * square))
                    gate = 0.5 + 0.5 * tangent
                    own = xs[R, R + i * CELL + x].astype(f32)
                    actives.append((own + v * gate).astype(bf16))
                    slope = gate + v * (gate - gate * gate) * (
                        2.0 * root_scale + 6.0 * root_scale * cubic_term * square
                    )
                    grad = (upstream[x].astype(f32) * slope).astype(bf16)
                    hs[R, R + i * CELL + x] = grad
                    total = total + grad.astype(f32)
        pooled[:, pl.ds(i * N, N)] = total
        obuf[:, rows16, :] = jnp.swapaxes(jnp.stack(actives), 0, 1)

    def weigh(o, half):
        groups = [half * (N // GROUP // 2) + i for i in range(N // GROUP // 2)]
        left = jnp.concatenate(
            [xs[o, pl.ds(i * GROUP, BAND)].reshape(BAND * C, N) for i in groups], axis=1
        )
        right = jnp.concatenate(
            [hs[R, pl.ds(R + i * GROUP, GROUP)].reshape(GROUP * C, N) for i in groups], axis=1
        )
        return dot(left, right, NT)

    for i in range(B // 2):
        near_field(B + 2 * i)
        near_field(B + 2 * i + 1)
        forward(i)
    for i in range(B // 2):
        grads[i] = weigh(i, 0)
        forward(B // 2 + i)

    one = split_dot(pooled[...], spread[...], NT)
    one_ref[...] = one
    for o in range(W):
        grads[o] = weigh(o, 1) + (grads[o] if o < B // 2 else weigh(o, 0))
        for i in range(2 * o, min(2 * o + 2, B)):
            pack_edges(hs[R, pl.ds(R + i * CELL, CELL)], i, hpack)
    def stencil_grad(p, carry):
        a = p // W
        b = lax.rem(p, W)
        part = [
            grads[b, pl.ds(pl.multiple_of((a + s) * C, C), C), pl.ds((s // 2) * N, N)]
            for s in range(GROUP)
        ]
        both = jnp.where(low, part[0] + part[2], part[1] + part[3])
        both = both + pltpu.roll(both, C, 1)
        stencil[p] = jnp.where(low[:32], both[:32], both[32:])
        return carry

    lax.fori_loop(0, W * W, stencil_grad, 0, unroll=True)

    for k in range(K):
        rs_src[k, pl.ds(0, 32), :] = stencil[(spots[0, k] + R) * W + spots[1, k] + R].astype(bf16)

    def link_grads(l, carry):
        grad = dot_split(picked[l], one_ref[...], NT)
        for half in range(2):
            rows = [grad[(2 * half + n) * 16 : (2 * half + n + 1) * 16] for n in range(2)]
            rs_src[2 * l + half, pl.ds(32, 16), :] = jnp.concatenate(
                [rows[0][:, :C], rows[1][:, :C]], axis=1
            ).astype(bf16)
        return carry

    lax.fori_loop(0, L, link_grads, 0, unroll=True)
    rs1[gy] = rs_src[gy]
    r1_start, r1_wait = line("gy", lambda p: rs_src.at[p], lambda p: rs1.at[p], r1_s, r1_r)
    r1_start()
    hhalo = halo_copies(hs, hpack, hright, hleft, hhalo_s, hhalo_r)
    for copy in hhalo:
        copy.start()
    two1[gy] = as_row(one_ref[...])
    u1_start, u1_wait = line("gy", lambda p: two1.at[gy], lambda p: two1.at[p], u1_s, u1_r)
    u1_start()

    def push(l, total):
        grad = one_ref[...]
        pushed = dot_split(lw[l], grad)
        return total + split_dot(pushed, onehot[l], NT, 2)

    pushes = lax.fori_loop(0, L, push, jnp.zeros((C, TARGETS), f32), unroll=True)
    for j in range(5):
        ctr[j] = pushes[:, j * N : (j + 1) * N]
    push_copies = []
    for n, (dx, dy) in enumerate(around()):
        slot = (1 - dx) * 3 + (1 - dy)
        copy = pltpu.make_async_remote_copy(
            src_ref=ctr.at[(8 - slot) // 2], dst_ref=rctr.at[slot], send_sem=ct_s.at[n],
            recv_sem=ct_r.at[n], device_id=at(dx, dy), device_id_type=MESH,
        )
        copy.start()
        push_copies.append(copy)

    r1_wait()
    total = rs1[0].astype(f32)
    for j in range(1, ny):
        total = total + rs1[j].astype(f32)
    rs2[gx] = total.astype(bf16)
    r2_start, r2_wait = line("gx", lambda p: rs2.at[gx], lambda p: rs2.at[p], r2_s, r2_r)
    r2_start()
    u1_wait()
    two2[gx] = two1[:, 0, :]
    u2_start, u2_wait = line("gx", lambda p: two2.at[gx], lambda p: two2.at[p], u2_s, u2_r)
    u2_start()

    for copy in hhalo:
        copy.wait()
    finish_halo(hs, hright, hleft)

    for copy in push_copies:
        copy.wait()
    evens = ctr[2]
    odds = jnp.zeros((C, N), f32)
    for slot in range(9):
        if slot == 4:
            continue
        if slot % 2 == 0:
            evens = evens + rctr[slot]
        else:
            odds = odds + rctr[slot]
    collected = evens + pltpu.roll(odds, C, 1)
    r2_wait()
    total = rs2[0].astype(f32)
    for j in range(1, nx):
        total = total + rs2[j].astype(f32)
    ag[gy] = total.astype(bf16)
    a1_start, a1_wait = line("gy", lambda p: ag.at[gy], lambda p: ag.at[p], a1_s, a1_r)
    a1_start()
    u2_wait()
    two_all = two2[...].reshape(N, N)[:, :C]
    kernel_grad = dot(tk[...], two_all, TN, HIGHEST)
    top_all = top2[...].reshape(N, N)
    top_out[...] = dot(top_all[:, :C], kernel_grad, TN, HIGHEST)
    mine = lax.broadcasted_iota(jnp.int32, (N, C), 0) == me
    kernel_row = jnp.sum(jnp.where(mine, kernel_grad, 0.0), axis=0, keepdims=True)
    top_coef_grad = jnp.sum(tw[...].astype(f32) * kernel_row, axis=1, keepdims=True)
    coarse_grad = (collected + top_coef_grad / B) / CELL
    spread_grad = split_dot(coarse_grad[:, :C], spread[pl.ds(0, C), :])
    for i in range(B):
        base[i] = spread_grad[:, i * N : (i + 1) * N]

    def backward(i, carry):
        rows16 = pl.ds(pl.multiple_of(i * CELL, CELL), CELL)
        shared = base[i]
        sums = []
        for half in range(2):
            near = banded(bwd, hs, i * 2 + half)
            for g in range(2):
                for s in range(GROUP):
                    sums.append(near[s * C : (s + 1) * C, g * N : (g + 1) * N] + shared)
        total = jnp.swapaxes(jnp.stack(sums), 0, 1)
        ibuf[:, rows16, :] = (cbuf[:, rows16, :].astype(f32) + total).astype(bf16)
        return carry

    lax.fori_loop(0, B, backward, 0, unroll=True)
    a1_wait()
    for k in range(K):
        whole = ag[k].astype(f32)
        near_out[k, pl.ds(0, 32), :] = whole[:32, :C]
        near_out[k, pl.ds(32, 32), :] = pltpu.roll(whole[:32], C, 1)[:, :C]
        link_out[k // 2, pl.ds((k % 2) * 32, 16), :] = whole[32:, :C]
        link_out[k // 2, pl.ds((k % 2) * 32 + 16, 16), :] = pltpu.roll(whole[32:], C, 1)[:, :C]


def store(*refs):
    count = len(refs) // 2
    sems = refs[-1]
    copies = []
    for n in range(count):
        pieces = 4 if n < 2 else 1
        size = refs[n].shape[0] // pieces
        for piece in range(pieces):
            rows = pl.ds(piece * size, size)
            copies.append(
                pltpu.make_async_copy(
                    refs[n].at[rows], refs[count + n].at[rows], sems.at[len(copies)]
                )
            )
    for copy in copies:
        copy.start()
    for copy in copies:
        copy.wait()


def solution(mesh):
    nx, ny = mesh.shape["gx"], mesh.shape["gy"]
    vmem = pl.BlockSpec(memory_space=pltpu.VMEM)
    anywhere = pl.BlockSpec(memory_space=pl.ANY)
    dma = pltpu.SemaphoreType.DMA

    def per_device(feat, cot, offsets, adjacency, near_w, link_w, top_w, top_k):
        scratch = [
            pltpu.VMEM((C, N, N), bf16),
            pltpu.VMEM((C, N, N), bf16),
            pltpu.VMEM((B, L, N), jnp.int32),
            pltpu.VMEM((2, K), jnp.int32),
            pltpu.VMEM((K, C, C), bf16),
            pltpu.VMEM((L, C, C), bf16),
            pltpu.VMEM((C, C), bf16),
            pltpu.VMEM((N, N), f32),
            pltpu.VMEM((W, HALO, C, N), bf16),
            pltpu.VMEM((W, HALO, C, N), bf16),
            pltpu.VMEM((2, 2, C, N), bf16),
            pltpu.VMEM((2, 2, C, N), bf16),
            pltpu.VMEM((4, C, N), bf16),
            pltpu.VMEM((4, C, N), bf16),
            pltpu.VMEM((4, C, N), bf16),
            pltpu.VMEM((4, C, N), bf16),
            pltpu.VMEM((K, C, N), f32),
            pltpu.VMEM((K, C, N), f32),
            pltpu.VMEM((W * W, C, N), bf16),
            pltpu.VMEM((W * W, C, N), bf16),
            pltpu.VMEM((GROUP * C, W * BAND * C), bf16),
            pltpu.VMEM((GROUP * C, W * BAND * C), bf16),
            pltpu.VMEM((N, B * N), bf16),
            pltpu.VMEM((C, B * N), f32),
            pltpu.VMEM((L, TARGETS, N), bf16),
            pltpu.VMEM((L, N), jnp.int32),
            pltpu.VMEM((9, C, N), bf16),
            pltpu.VMEM((L, C, N), bf16),
            pltpu.VMEM((B, C, N), f32),
            pltpu.VMEM((ny, 8, N), f32),
            pltpu.VMEM((nx, ny, N), f32),
            pltpu.VMEM((ny, 8, N), f32),
            pltpu.VMEM((nx, ny, N), f32),
            pltpu.VMEM((5, C, N), f32),
            pltpu.VMEM((9, C, N), f32),
            pltpu.VMEM((W, BAND * C, GROUP * C), f32),
            pltpu.VMEM((ny, 48, N), bf16),
            pltpu.VMEM((ny, 48, N), bf16),
            pltpu.VMEM((nx, 48, N), bf16),
            pltpu.VMEM((ny, 48, N), bf16),
            pltpu.VMEM((C, N), f32),
            pltpu.VMEM((K, N), jnp.int32),
            pltpu.VMEM((2 * N, 4 * N), bf16),
            pltpu.VMEM((8, C, N), bf16),
            pltpu.VMEM((N // (2 * GROUP), GROUP * C, 2 * N), f32),
            pltpu.VMEM((W * W, 32, N), f32),
            dma((11,)),
            dma((8,)), dma((8,)), dma((8,)), dma((8,)),
            dma((8,)), dma((8,)), dma((8,)), dma((8,)),
            dma((ny,)), dma((ny,)), dma((nx,)), dma((nx,)),
            dma((ny,)), dma((ny,)), dma((nx,)), dma((nx,)),
            dma((ny,)), dma((ny,)), dma((nx,)), dma((nx,)), dma((ny,)), dma((ny,)),
        ]
        results = (
            ((C, N, N), bf16),
            ((C, N, N), bf16),
            ((K, C, C), f32),
            ((L, C, C), f32),
            ((C, C), f32),
        )
        held = pl.pallas_call(
            functools.partial(kernel, nx, ny),
            out_shape=[pltpu.VMEM(*result) for result in results],
            in_specs=[
                anywhere, anywhere, anywhere, anywhere,
                pl.BlockSpec(memory_space=pltpu.SMEM),
                anywhere, anywhere, anywhere, anywhere,
            ],
            out_specs=[vmem] * 5,
            scratch_shapes=scratch,
            compiler_params=pltpu.CompilerParams(
                collective_id=0, has_side_effects=True, vmem_limit_bytes=54 * 2**20
            ),
        )(
            feat, cot, jnp.transpose(adjacency, (0, 2, 1)), offsets.T, offsets.T, near_w, link_w,
            top_w, top_k,
        )
        return pl.pallas_call(
            store,
            out_shape=[jax.ShapeDtypeStruct(*result) for result in results],
            in_specs=[vmem] * 5,
            out_specs=[anywhere] * 5,
            scratch_shapes=[dma((11,))],
            compiler_params=pltpu.CompilerParams(vmem_limit_bytes=2**20),
        )(*[pltpu.with_memory_space_constraint(value, pltpu.VMEM) for value in held])

    return jax.shard_map(
        per_device,
        mesh=mesh,
        in_specs=(P(None, "gx", "gy"), P(None, "gx", "gy"), P(), P(), P(), P(), P(), P()),
        out_specs=(P(None, "gx", "gy"), P(None, "gx", "gy"), P(), P(), P()),
        check_vma=False,
    )
```
